128 devices in a mesh: gx: 8 (over x, core), gy: 16 (over y, z).
Axes of the slice: x: 4, y: 4, z: 4, core: 2. Of those that a mesh axis runs over, the one named last changes fastest.
Arguments:
- fields: float32 [512, 2048, 256], P('gx', 'gy'), may hold values from -4 to 4
- increments: bfloat16 [512, 2048, 256], P('gx', 'gy'), may hold values from -5 to 5
- flow_field: float32 [6, 512, 2048], P(None, 'gx', 'gy'), may hold values from -4 to 4
- brick_owner: int32 [16, 64], P('gx', 'gy'), may hold values from -1 to 895, as said below
Outputs:
- relaid: float32 [896, 32, 32, 256], P(('gx', 'gy'))
The draws below stay inside these ranges and needn't reach their ends.
Inputs may be any that keep to these rules, and one draw needn't show every extreme that they name: `brick_owner`: -1 marks a solid brick. Every slot 0 to 895 is named by exactly one brick; a slot s lies on device s // 7 counted gx-major. Each brick's owner device has the same gx index as the device that holds the brick in the slab. No two bricks of one device of the slab share an owner device. In every index of gx some device of the slab holds 8 fluid bricks.
All inputs are finite; a program needn't handle non-finite values.
Results may differ from the reference program's by a relative error of at most 0.0003.
Values may be sent and summed in bfloat16 or wider, within the bound.
A program may use at most 192 MiB of HBM per device.

```python
import math
import jax
import jax.numpy as jnp
from jax import lax

BRICK = 32
ROWS_DEV = 2
COLS_DEV = 4
LAYERS = 8
FIELDS = 32
CAPACITY = 7
BRICK_ROWS = 16
BRICK_COLS = 64
CELLS_X = 512
CELLS_Y = 2048
SLOTS = 896


def draw_brick_owner(key, part):
    groups = BRICK_ROWS // ROWS_DEV
    peer_count = BRICK_COLS // COLS_DEV
    span_cols = 8 * COLS_DEV
    places = BRICK_COLS // span_cols

    def one_group(group_index):
        group_key = jax.random.fold_in(key, group_index)
        key_list = jax.random.split(group_key, 4)
        starts = jax.random.randint(key_list[0], (places,), 0, span_cols - COLS_DEV + 1)
        offset = jax.random.randint(key_list[1], (), 0, span_cols)
        column = jnp.arange(BRICK_COLS, dtype=jnp.int32)
        shifted = (column - offset) % BRICK_COLS
        which = shifted // span_cols
        inner = shifted % span_cols
        begin = jnp.take(starts, which)
        solid_cols = jnp.logical_and(inner >= begin, inner < begin + COLS_DEV)
        fluid_grid = jnp.broadcast_to(jnp.logical_not(solid_cols)[:, None], (BRICK_COLS, ROWS_DEV))
        fluid_flat = fluid_grid.reshape(-1).astype(jnp.int32)
        fluid_rank = jnp.cumsum(fluid_flat) - 1
        shuffle = jax.random.permutation(key_list[2], peer_count)
        rotation = jax.random.randint(key_list[3], (peer_count,), 0, CAPACITY)
        target = jnp.take(shuffle, fluid_rank % peer_count)
        place_in = (fluid_rank // peer_count + jnp.take(rotation, target)) % CAPACITY
        owner_slot = (group_index * peer_count + target) * CAPACITY + place_in
        owner_slot = jnp.where(fluid_flat > 0, owner_slot, -1)
        return owner_slot.reshape(BRICK_COLS, ROWS_DEV).T
    result = jax.vmap(one_group)(jnp.arange(groups, dtype=jnp.int32))
    return result.reshape(BRICK_ROWS, BRICK_COLS).astype(jnp.int32)


def block_scale(key, dims, cuts, low, high):
    factor_of, own = 1.0, jax.random.fold_in(key, 6)
    for dim, blocks in cuts:
        heights = jnp.exp(jax.random.uniform(jax.random.fold_in(own, dim), (blocks,), jnp.float32, low / len(cuts), high / len(cuts)))
        factor_of = factor_of * jnp.repeat(heights, dims[dim] // blocks).reshape([-1 if axis == dim else 1 for axis in range(len(dims))])
    return factor_of


def bell_draw(rng, extent, scale, bound, cuts=(), kind=jnp.bfloat16):
    entries = jax.random.normal(rng, extent, jnp.float32) * scale
    if len(cuts) > 0:
        entries = block_scale(rng, extent, cuts, -0.22, 0.18) * entries
    return jnp.clip(entries, min=-bound, max=bound).astype(kind)


def setup_inputs(seed: int = 0) -> dict:
    key_of = jax.random.split(jax.random.key(seed), 5)
    fields = jnp.clip(jax.random.uniform(key_of[0], (CELLS_X, CELLS_Y, LAYERS * FIELDS), jnp.float32, -4.0, 4.0) * block_scale(key_of[0], (CELLS_X, CELLS_Y, LAYERS * FIELDS), ((0, 8), (1, 16)), -0.4, 0.0), -4.0, 4.0)
    increments = bell_draw(key_of[1], (CELLS_X, CELLS_Y, LAYERS * FIELDS), 1.0, 5.0, ((0, 8), (1, 16)))
    flow_field = bell_draw(key_of[2], (6, CELLS_X, CELLS_Y), 1.0, 4.0, ((1, 8), (2, 16)), jnp.float32)
    brick_owner = draw_brick_owner(jax.random.fold_in(key_of[4], 71), 0)
    return dict(fields=fields, increments=increments, flow_field=flow_field, brick_owner=brick_owner)


TIME_STEP = 0.1
NOISE_SCALE = math.sqrt(0.1)
FENE_LIMIT = 25.0
SPRING_FLOOR = 0.1

def reference(fields, increments, flow_field, brick_owner):
    live_brick = (brick_owner >= 0).astype(jnp.float32)
    cell_live = jnp.repeat(jnp.repeat(live_brick, BRICK, 0), BRICK, 1)
    masked = fields * cell_live[:, :, None]
    half_lanes = FIELDS // 2
    layered = jnp.moveaxis(masked.reshape(CELLS_X, CELLS_Y, 2, LAYERS, half_lanes), 3, 0)
    kicked = jnp.moveaxis(increments.reshape(CELLS_X, CELLS_Y, 2, LAYERS, half_lanes), 3, 0)
    speed_x = flow_field[0][:, :, None, None]
    speed_y = flow_field[1][:, :, None, None]
    grad_one = flow_field[2][:, :, None]
    grad_two = flow_field[3][:, :, None]
    grad_three = flow_field[4][:, :, None]
    grad_four = flow_field[5][:, :, None]

    def advance(operands):
        layer_state, layer_kick = operands
        back_x = 1.5 * layer_state - 2.0 * jnp.roll(layer_state, 1, 0) + 0.5 * jnp.roll(layer_state, 2, 0)
        ahead_x = -1.5 * layer_state + 2.0 * jnp.roll(layer_state, -1, 0) - 0.5 * jnp.roll(layer_state, -2, 0)
        back_y = 1.5 * layer_state - 2.0 * jnp.roll(layer_state, 1, 1) + 0.5 * jnp.roll(layer_state, 2, 1)
        ahead_y = -1.5 * layer_state + 2.0 * jnp.roll(layer_state, -1, 1) - 0.5 * jnp.roll(layer_state, -2, 1)
        transport = jnp.maximum(speed_x, 0.0) * back_x + jnp.minimum(speed_x, 0.0) * ahead_x + jnp.maximum(speed_y, 0.0) * back_y + jnp.minimum(speed_y, 0.0) * ahead_y
        first_part = layer_state[:, :, 0]
        second = layer_state[:, :, 1]
        spring = 1.0 / jnp.maximum(1.0 - (first_part * first_part + second * second) / FENE_LIMIT, SPRING_FLOOR)
        drift_a = grad_one * first_part + grad_two * second - 0.5 * spring * first_part
        drift_b = grad_three * first_part + grad_four * second - 0.5 * spring * second
        drift = jnp.stack([drift_a, drift_b], axis=2)
        return layer_state - TIME_STEP * transport + TIME_STEP * drift + NOISE_SCALE * layer_kick.astype(jnp.float32)
    moved = lax.map(advance, (layered, kicked))
    advanced = jnp.moveaxis(moved, 0, 3).reshape(CELLS_X, CELLS_Y, LAYERS * FIELDS)
    bricks = advanced.reshape(BRICK_ROWS, BRICK, BRICK_COLS, BRICK, LAYERS * FIELDS)
    bricks = bricks.transpose(0, 2, 1, 3, 4).reshape(BRICK_ROWS * BRICK_COLS, BRICK, BRICK, LAYERS * FIELDS)
    owner_flat = brick_owner.reshape(-1)
    spots = jnp.where(owner_flat >= 0, owner_flat, SLOTS).astype(jnp.int32)
    holder = jnp.zeros((SLOTS,), jnp.int32).at[spots].set(jnp.arange(BRICK_ROWS * BRICK_COLS, dtype=jnp.int32), mode='drop')
    return jnp.take(bricks, holder, axis=0)
```

```python
import functools
import math

import jax
import jax.numpy as jnp
from jax import lax
from jax.experimental import pallas as pl
from jax.experimental.pallas import tpu as pltpu
from jax.sharding import PartitionSpec as P

MESH = pl.DeviceIdType.MESH
NOISE_SCALE = math.sqrt(0.1)
CODE_MAX = 32767.0
VALUE_MAX = 24.0
EDGE = 32
PITCH = 144
NX, NY = 64, 128


def encode(value):
    root = jnp.maximum(jnp.abs(value), 1e-30) * (1.0 / VALUE_MAX)
    for _ in range(3):
        root = root * lax.rsqrt(root)
    code = jnp.minimum(root * CODE_MAX + 0.5, CODE_MAX)
    return jnp.where(value < 0.0, -code, code).astype(jnp.int32).astype(jnp.int16)


def decode(code):
    part = code.astype(jnp.float32)
    square = part * (1.0 / CODE_MAX)
    square = square * square
    square = square * square
    square = square * square * VALUE_MAX
    return jnp.where(part < 0.0, -square, square)


def live_of(owner, row, col):
    return jnp.where(owner[row, col] >= 0, 1.0, 0.0).astype(jnp.float32)


def start_loads(fields, incr, flow, F, NZ, FL, xs, ye, lsem):
    copies = []
    k = 0
    edges = []
    for side in range(2):
        for comp in range(2):
            lanes = pl.ds(128 * comp, 128)
            edges.append((fields.at[pl.ds(62 * side, 2), :, lanes], xs.at[side, comp]))
            edges.append((fields.at[:, pl.ds(120 * side, 8), lanes], ye.at[side, comp]))
    for src, dst in edges:
        copies.append(pltpu.make_async_copy(src, dst, lsem.at[k]))
        k += 1
    copies.append(pltpu.make_async_copy(flow, FL, lsem.at[k]))
    k += 1
    for comp in range(2):
        copies.append(
            pltpu.make_async_copy(
                fields.at[:, :, pl.ds(128 * comp, 128)],
                F.at[comp, pl.ds(2, NX), pl.ds(8, NY)],
                lsem.at[k],
            )
        )
        k += 1
    copies.append(pltpu.make_async_copy(incr, NZ, lsem.at[k]))
    for copy in copies:
        copy.start()
    return copies[:8], copies[8:9], copies[9:11], copies[11:]


def mask_edges(owner, xs, ye, ys):
    for side in range(2):
        for comp in range(2):
            for col in range(4):
                part = pl.ds(EDGE * col, EDGE)
                live = live_of(owner, side, col)
                for line in range(2):
                    xs[side, comp, line, part, :] = xs[side, comp, line, part, :] * live
    for side in range(2):
        for row in range(2):
            live = live_of(owner, row, 3 * side)
            for comp in range(2):
                strip = ye.at[side, comp].reshape(NX * 8, 128)
                for line in range(2):
                    for g in range(4):
                        x0 = EDGE * row + 8 * g
                        ys[side, comp, line, pl.ds(x0, 8), :] = (
                            strip[pl.ds(x0 * 8 + 6 * side + line, 8, stride=8), :] * live
                        )


def halo_copies(F, xs, ys, yr, hs, hr):
    gx, gy = lax.axis_index("gx"), lax.axis_index("gy")
    copies = []
    for side in range(2):
        step = 2 * side - 1
        tx = lax.rem(gx + step + 8, 8)
        ty = lax.rem(gy + step + 16, 16)
        copies.append(
            pltpu.make_async_remote_copy(
                xs.at[side],
                F.at[:, pl.ds(66 * (1 - side), 2), pl.ds(8, NY)],
                hs.at[side],
                hr.at[side],
                device_id=(tx, gy),
                device_id_type=MESH,
            )
        )
        copies.append(
            pltpu.make_async_remote_copy(
                ys.at[side],
                yr.at[side],
                hs.at[2 + side],
                hr.at[2 + side],
                device_id=(gx, ty),
                device_id_type=MESH,
            )
        )
    return copies


def make_coefficients(FL, CT):
    u, v = FL[0], FL[1]
    up, un = jnp.maximum(u, 0.0), jnp.minimum(u, 0.0)
    vp, vn = jnp.maximum(v, 0.0), jnp.minimum(v, 0.0)
    keep = 1.0 - 0.15 * ((up - un) + (vp - vn))
    channels = [
        keep + 0.1 * FL[2],
        0.1 * FL[3],
        0.1 * FL[4],
        keep + 0.1 * FL[5],
        0.2 * up,
        -0.2 * un,
        0.2 * vp,
        -0.2 * vn,
    ]
    for g in range(4):
        block = jnp.concatenate([c[16 * g : 16 * g + 16] for c in channels], axis=0)
        CT[g] = block.T


def mask_block(owner, F2):
    for row in range(2):
        for col in range(4):
            live = live_of(owner, row, col)

            def line(x, carry):
                part = pl.ds((2 + EDGE * row + x) * PITCH + 8 + EDGE * col, EDGE)
                for comp in range(2):
                    F2[comp, part, :] = F2[comp, part, :] * live
                return carry

            lax.fori_loop(0, EDGE, line, 0, unroll=2)


def unpack_halo(F2, yr):
    for side in range(2):
        for comp in range(2):
            for line in range(2):
                place = 6 + line if side == 1 else 136 + line
                for g in range(8):
                    F2[comp, pl.ds((2 + 8 * g) * PITCH + place, 8, stride=PITCH), :] = yr[
                        side, comp, line, pl.ds(8 * g, 8), :
                    ]


def brick_line(F2, NZ, CT, row, col, x):
    line = EDGE * row + x
    base = (2 + line) * PITCH + 8 + EDGE * col
    ys = pl.ds(pl.multiple_of(EDGE * col, EDGE), EDGE)
    table = CT[line // 16, ys, :]
    spot = jnp.full((EDGE, 128), lax.rem(line, 16), jnp.int32)
    c = [jnp.take_along_axis(table, spot + 16 * k, axis=1) for k in range(8)]
    q = [F2[comp, pl.ds(base, EDGE), :] for comp in range(2)]
    rest = jnp.maximum(20.0 - 0.8 * (q[0] * q[0] + q[1] * q[1]), 2.0)
    soft = pl.reciprocal(rest, approx=True)
    soft = soft * (2.0 - rest * soft)
    out = []
    for comp in range(2):

        def at(shift):
            return F2[comp, pl.ds(base + shift, EDGE), :]

        moved = c[4] * (at(-PITCH) - 0.25 * at(-2 * PITCH))
        moved += c[5] * (at(PITCH) - 0.25 * at(2 * PITCH))
        moved += c[6] * (at(-1) - 0.25 * at(-2))
        moved += c[7] * (at(1) - 0.25 * at(2))
        own, cross = (c[0], c[1]) if comp == 0 else (c[3], c[2])
        noise = NZ[line, ys, pl.ds(128 * comp, 128)].astype(jnp.float32)
        total = (own - soft) * q[comp] + cross * q[1 - comp] + moved + NOISE_SCALE * noise
        out.append(encode(total))
    return out


def step_kernel(
    owner, fields, incr, flow, out, F, NZ, FL, CT, xs, ye, ys, yr, codes, lsem, hs, hr, osem
):
    gx, gy = lax.axis_index("gx"), lax.axis_index("gy")
    edges, flows, block, noise = start_loads(fields, incr, flow, F, NZ, FL, xs, ye, lsem)
    barrier = pltpu.get_barrier_semaphore()
    for step in (1, -1):
        for target in (
            (lax.rem(gx + step + 8, 8), gy),
            (gx, lax.rem(gy + step + 16, 16)),
        ):
            pl.semaphore_signal(barrier, inc=1, device_id=target, device_id_type=MESH)
    for copy in edges:
        copy.wait()
    mask_edges(owner, xs, ye, ys)
    pl.semaphore_wait(barrier, 4)
    halos = halo_copies(F, xs, ys, yr, hs, hr)
    for copy in halos:
        copy.start()
    F2 = F.reshape(2, 68 * PITCH, 128)
    for copy in flows:
        copy.wait()
    make_coefficients(FL, CT)
    for copy in block:
        copy.wait()
    mask_block(owner, F2)
    for copy in noise:
        copy.wait()
    for copy in halos:
        copy.wait()
    unpack_halo(F2, yr)

    def brick(b, carry):
        row, col = b // 4, lax.rem(b, 4)

        def line(x, inner):
            coded = brick_line(F2, NZ, CT, row, col, x)
            for comp in range(2):
                codes[b, pl.ds(pl.multiple_of(x * EDGE, EDGE), EDGE), pl.ds(128 * comp, 128)] = coded[comp]
            return inner

        lax.fori_loop(0, EDGE, line, 0)
        pltpu.make_async_copy(codes.at[b], out.at[b], osem.at[b]).start()
        return carry

    lax.fori_loop(0, 8, brick, 0)
    for b in range(8):
        pltpu.make_async_copy(codes.at[b], out.at[b], osem.at[b]).wait()


def advance(fields, increments, flow_field, brick_owner):
    any_ = pl.BlockSpec(memory_space=pl.ANY)
    return pl.pallas_call(
        step_kernel,
        out_shape=jax.ShapeDtypeStruct((8, EDGE * EDGE, 256), jnp.int16),
        in_specs=[pl.BlockSpec(memory_space=pltpu.SMEM), any_, any_, any_],
        out_specs=any_,
        scratch_shapes=[
            pltpu.VMEM((2, 68, PITCH, 128), jnp.float32),
            pltpu.VMEM((NX, NY, 256), jnp.bfloat16),
            pltpu.VMEM((6, NX, NY), jnp.float32),
            pltpu.VMEM((4, 128, 128), jnp.float32),
            pltpu.VMEM((2, 2, 2, NY, 128), jnp.float32),
            pltpu.VMEM((2, 2, NX, 8, 128), jnp.float32),
            pltpu.VMEM((2, 2, 2, NX, 128), jnp.float32),
            pltpu.VMEM((2, 2, 2, NX, 128), jnp.float32),
            pltpu.VMEM((8, EDGE * EDGE, 256), jnp.int16),
            pltpu.SemaphoreType.DMA((12,)),
            pltpu.SemaphoreType.DMA((4,)),
            pltpu.SemaphoreType.DMA((4,)),
            pltpu.SemaphoreType.DMA((8,)),
        ],
        compiler_params=pltpu.CompilerParams(
            collective_id=0, has_side_effects=True, vmem_limit_bytes=56 * 2**20
        ),
    )(brick_owner, fields, increments, flow_field)


def finish_kernel(source, codes, out):
    out[0] = decode(codes[0]).reshape(out.shape[1:])


def finish(source, arrived, slots):
    return pl.pallas_call(
        finish_kernel,
        out_shape=jax.ShapeDtypeStruct((slots, EDGE, EDGE, 256), jnp.float32),
        grid_spec=pltpu.PrefetchScalarGridSpec(
            num_scalar_prefetch=1,
            grid=(slots, 2),
            in_specs=[pl.BlockSpec((1, 512, 256), lambda s, h, source: (source[s], h, 0))],
            out_specs=pl.BlockSpec((1, 16, EDGE, 256), lambda s, h, source: (s, h, 0, 0)),
        ),
        compiler_params=pltpu.CompilerParams(vmem_limit_bytes=32 * 2**20),
    )(source, arrived)


def pick_kernel(chosen, codes, out):
    out[...] = codes[...]


def pick(chosen, codes, peers):
    block = (1, EDGE * EDGE, 256)
    return pl.pallas_call(
        pick_kernel,
        out_shape=jax.ShapeDtypeStruct((peers, EDGE * EDGE, 256), jnp.int16),
        grid_spec=pltpu.PrefetchScalarGridSpec(
            num_scalar_prefetch=1,
            grid=(peers,),
            in_specs=[pl.BlockSpec(block, lambda s, chosen: (chosen[s], 0, 0))],
            out_specs=pl.BlockSpec(block, lambda s, chosen: (s, 0, 0)),
        ),
        compiler_params=pltpu.CompilerParams(vmem_limit_bytes=32 * 2**20),
    )(chosen, codes)


def on_device(fields, increments, flow_field, brick_owner):
    slot_count = 7
    peer_count = lax.axis_size("gy")
    owner_table = lax.all_gather(brick_owner, "gy", axis=1, tiled=True)
    device = lax.axis_index("gx") * peer_count + lax.axis_index("gy")
    owner_flat = brick_owner.reshape(8)
    target = jnp.where(owner_flat >= 0, owner_flat // slot_count % peer_count, -1)
    match_grid = target[None, :] == jnp.arange(peer_count, dtype=jnp.int32)[:, None]
    chosen = jnp.sum(jnp.where(match_grid, jnp.arange(8, dtype=jnp.int32)[None, :], 0), axis=1)
    wanted = device * slot_count + jnp.arange(slot_count, dtype=jnp.int32)
    column = jnp.arange(owner_table.shape[1], dtype=jnp.int32)
    found = owner_table[None, :, :] == wanted[:, None, None]
    source = jnp.sum(jnp.where(found, (column // 4)[None, None, :], 0), axis=(1, 2))
    codes = advance(fields, increments, flow_field, brick_owner)
    picked = pick(chosen, codes, peer_count)
    arrived = lax.all_to_all(picked, "gy", split_axis=0, concat_axis=0, tiled=True)
    return finish(source, arrived, slot_count)


def solution(mesh):
    in_specs = (P("gx", "gy", None), P("gx", "gy", None), P(None, "gx", "gy"), P("gx", "gy"))
    out_specs = P(("gx", "gy"), None, None, None)
    return jax.shard_map(
        on_device, mesh=mesh, in_specs=in_specs, out_specs=out_specs, check_vma=False
    )
```

```python
import functools
import math

import jax
import jax.numpy as jnp
from jax import lax
from jax.experimental import pallas as pl
from jax.experimental.pallas import tpu as pltpu
from jax.sharding import PartitionSpec as P

MESH = pl.DeviceIdType.MESH
NOISE_SCALE = math.sqrt(0.1)
CODE_MAX = 32767.0
VALUE_MAX = 24.0
EDGE = 32
PITCH = 144
NX, NY = 64, 128
CAPACITY = 7
PIECES = 4
OWN = 8 * PIECES
ROUNDS = 25


def encode(value):
    root = jnp.maximum(jnp.abs(value), 1e-30) * (1.0 / VALUE_MAX)
    for _ in range(3):
        root = root * lax.rsqrt(root)
    code = jnp.minimum(root * CODE_MAX + 0.5, CODE_MAX)
    return jnp.where(value < 0.0, -code, code).astype(jnp.int32).astype(jnp.int16)


def decode(code):
    part = code.astype(jnp.float32)
    square = part * (1.0 / CODE_MAX)
    square = square * square
    square = square * square
    square = square * square * VALUE_MAX
    return jnp.where(part < 0.0, -square, square)


def live_of(owner, row, col):
    return jnp.where(owner[row, col] >= 0, 1.0, 0.0).astype(jnp.float32)


def start_loads(fields, incr, flow, F, NZ, FL, xs, ye, lsem):
    copies = []
    k = 0
    edges = []
    for side in range(2):
        for comp in range(2):
            lanes = pl.ds(128 * comp, 128)
            edges.append((fields.at[pl.ds(62 * side, 2), :, lanes], xs.at[side, comp]))
            edges.append((fields.at[:, pl.ds(120 * side, 8), lanes], ye.at[side, comp]))
    for src, dst in edges:
        copies.append(pltpu.make_async_copy(src, dst, lsem.at[k]))
        k += 1
    copies.append(pltpu.make_async_copy(flow, FL, lsem.at[k]))
    k += 1
    for comp in range(2):
        copies.append(
            pltpu.make_async_copy(
                fields.at[:, :, pl.ds(128 * comp, 128)],
                F.at[comp, pl.ds(2, NX), pl.ds(8, NY)],
                lsem.at[k],
            )
        )
        k += 1
    copies.append(pltpu.make_async_copy(incr, NZ, lsem.at[k]))
    for copy in copies:
        copy.start()
    return copies[:8], copies[8:9], copies[9:11], copies[11:]


def mask_edges(owner, xs, ye, ys):
    for side in range(2):
        for comp in range(2):
            for col in range(4):
                part = pl.ds(EDGE * col, EDGE)
                live = live_of(owner, side, col)
                for line in range(2):
                    xs[side, comp, line, part, :] = xs[side, comp, line, part, :] * live
    for side in range(2):
        for row in range(2):
            live = live_of(owner, row, 3 * side)
            for comp in range(2):
                strip = ye.at[side, comp].reshape(NX * 8, 128)
                for line in range(2):
                    for g in range(4):
                        x0 = EDGE * row + 8 * g
                        ys[side, comp, line, pl.ds(x0, 8), :] = (
                            strip[pl.ds(x0 * 8 + 6 * side + line, 8, stride=8), :] * live
                        )


def halo_copies(F, xs, ys, yr, hs, hr):
    gx, gy = lax.axis_index("gx"), lax.axis_index("gy")
    copies = []
    for side in range(2):
        step = 2 * side - 1
        tx = lax.rem(gx + step + 8, 8)
        ty = lax.rem(gy + step + 16, 16)
        copies.append(
            pltpu.make_async_remote_copy(
                xs.at[side],
                F.at[:, pl.ds(66 * (1 - side), 2), pl.ds(8, NY)],
                hs.at[side],
                hr.at[side],
                device_id=(tx, gy),
                device_id_type=MESH,
            )
        )
        copies.append(
            pltpu.make_async_remote_copy(
                ys.at[side],
                yr.at[side],
                hs.at[2 + side],
                hr.at[2 + side],
                device_id=(gx, ty),
                device_id_type=MESH,
            )
        )
    return copies


def make_coefficients(FL, CT):
    u, v = FL[0], FL[1]
    up, un = jnp.maximum(u, 0.0), jnp.minimum(u, 0.0)
    vp, vn = jnp.maximum(v, 0.0), jnp.minimum(v, 0.0)
    keep = 1.0 - 0.15 * ((up - un) + (vp - vn))
    channels = [
        keep + 0.1 * FL[2],
        0.1 * FL[3],
        0.1 * FL[4],
        keep + 0.1 * FL[5],
        0.2 * up,
        -0.2 * un,
        0.2 * vp,
        -0.2 * vn,
    ]
    for g in range(4):
        block = jnp.concatenate([c[16 * g : 16 * g + 16] for c in channels], axis=0)
        CT[g] = block.T


def mask_block(owner, F2):
    for row in range(2):
        for col in range(4):
            live = live_of(owner, row, col)

            def line(x, carry):
                part = pl.ds((2 + EDGE * row + x) * PITCH + 8 + EDGE * col, EDGE)
                for comp in range(2):
                    F2[comp, part, :] = F2[comp, part, :] * live
                return carry

            lax.fori_loop(0, EDGE, line, 0, unroll=2)


def unpack_halo(F2, yr):
    for side in range(2):
        for comp in range(2):
            for line in range(2):
                place = 6 + line if side == 1 else 136 + line
                for g in range(8):
                    F2[comp, pl.ds((2 + 8 * g) * PITCH + place, 8, stride=PITCH), :] = yr[
                        side, comp, line, pl.ds(8 * g, 8), :
                    ]


def brick_line(F2, NZ, CT, row, col, half, step):
    line = EDGE * row + 16 * half + step
    base = (2 + line) * PITCH + 8 + EDGE * col
    ys = pl.ds(pl.multiple_of(EDGE * col, EDGE), EDGE)
    table = CT[2 * row + half, ys, :]
    spots = [16 * k + step for k in range(8)]
    c = [jnp.broadcast_to(table[:, k : k + 1], (EDGE, 128)) for k in spots]
    q = [F2[comp, pl.ds(base, EDGE), :] for comp in range(2)]
    rest = jnp.maximum(20.0 - 0.8 * (q[0] * q[0] + q[1] * q[1]), 2.0)
    soft = pl.reciprocal(rest, approx=True)
    soft = soft * (2.0 - rest * soft)
    out = []
    for comp in range(2):

        def at(shift):
            return F2[comp, pl.ds(base + shift, EDGE), :]

        moved = c[4] * (at(-PITCH) - 0.25 * at(-2 * PITCH))
        moved += c[5] * (at(PITCH) - 0.25 * at(2 * PITCH))
        moved += c[6] * (at(-1) - 0.25 * at(-2))
        moved += c[7] * (at(1) - 0.25 * at(2))
        own, cross = (c[0], c[1]) if comp == 0 else (c[3], c[2])
        noise = NZ[line, ys, pl.ds(128 * comp, 128)].astype(jnp.float32)
        total = (own - soft) * q[comp] + cross * q[1 - comp] + moved + NOISE_SCALE * noise
        out.append(encode(total))
    return out


def slot_in_pool(number):
    return jnp.minimum(jnp.maximum(number, 0), OWN + 4 * ROUNDS - 1)


def make_tile(owner, gy):
    lane = lax.broadcasted_iota(jnp.int32, (8, 128), 1)
    brick = (lane % 32) // PIECES
    tile = jnp.zeros((8, 128), jnp.int32)
    for b in range(8):
        slot = jnp.maximum(owner[b // 4, b % 4], 0)
        code = lax.rem(slot // CAPACITY, 16) * 8 + lax.rem(slot, CAPACITY) + 1
        code = jnp.where(owner[b // 4, b % 4] >= 0, code, 0)
        tile = jnp.where(brick == b, code, tile)
    return jnp.where(lane // 32 == lax.rem(gy, 4), tile, 0)


def plan_routes(tiles, plan, last, flags, gx, gy):
    shape = (8, 512)
    p = lax.broadcasted_iota(jnp.int32, shape, 1)
    rowid = lax.broadcasted_iota(jnp.int32, (64, 512), 0)
    src, brick, piece = p // 32, (p // PIECES) % 8, p % PIECES
    code = jnp.concatenate(
        [tiles[4 * q] + tiles[4 * q + 1] + tiles[4 * q + 2] + tiles[4 * q + 3] for q in range(4)], axis=1
    )
    dest, slot = (jnp.maximum(code - 1, 0)) // 8, (jnp.maximum(code - 1, 0)) % 8
    live = code > 0
    y, z = src // 4, src % 4
    ty, tz = (dest // 4 - y + 4) % 4, (dest % 4 - z + 4) % 4
    tie = (piece + brick + src) % 2
    kz = jnp.where(tz == 2, tie, jnp.where(tz == 3, 1, 0))
    ky = jnp.where(ty == 2, tie, jnp.where(ty == 3, 1, 0))
    nz = jnp.where(live, jnp.where(tz == 3, 1, tz), 0)
    ny = jnp.where(live, jnp.where(ty == 3, 1, ty), 0)
    first = (piece // 2 + brick) % 2
    lane = lax.broadcasted_iota(jnp.int32, (8, 128), 1)
    mine = lax.rem(rowid[:, :1], 16) == gy

    def step(r, carry):
        nz, ny, y, z, loc, ready = carry
        usez = jnp.logical_and(nz > 0, jnp.logical_or(first == 0, ny == 0))
        dist = nz + ny
        active = jnp.logical_and(dist > 0, ready <= r)
        k = jnp.where(usez, kz, ky + 2)
        key = jnp.where(active, k * 16 + y * 4 + z, -1)
        score = dist * 512 + loc + 1
        key = jnp.concatenate([key] * 8, axis=0)
        wide = jnp.concatenate([score] * 8, axis=0)
        bids = jnp.where(rowid == key, wide, 0)
        best = jnp.maximum(jnp.max(bids, axis=1, keepdims=True), 1)
        won = jnp.where(bids == best, 1, 0)
        moved = won[0:8]
        for i in range(1, 8):
            moved = jnp.maximum(moved, won[8 * i : 8 * i + 8])
        moved = jnp.broadcast_to(jnp.max(moved, axis=0, keepdims=True), shape) > 0
        own = jnp.where(mine, best, 0)
        line = jnp.zeros((8, 128), jnp.int32)
        for i in range(4):
            pick = jnp.max(own[16 * i : 16 * i + 16], axis=0, keepdims=True)
            line = jnp.where(lane == i, jnp.broadcast_to(pick, (8, 128)), line)
        number = jnp.maximum(line - 1, 0) % 512
        plan[pl.ds(pl.multiple_of(8 * r, 8), 8), :] = number
        wentz = jnp.logical_and(moved, usez)
        wenty = jnp.logical_and(moved, jnp.logical_not(usez))
        nz = jnp.where(wentz, nz - 1, nz)
        ny = jnp.where(wenty, ny - 1, ny)
        z = jnp.where(wentz, (z + 5 - 2 * kz) % 4, z)
        y = jnp.where(wenty, (y + 5 - 2 * ky) % 4, y)
        loc = jnp.where(moved, OWN + 4 * r + k, loc)
        ready = jnp.where(moved, r + 2, ready)
        return nz, ny, y, z, loc, ready

    start = (nz, ny, y, z, brick * PIECES + piece, brick)
    nz, ny, y, z, loc, ready = lax.fori_loop(0, ROUNDS, step, start)
    row = lax.broadcasted_iota(jnp.int32, shape, 0)
    wanted = jnp.logical_and(live, jnp.logical_and(dest == gy, slot == row))
    for i in range(PIECES):
        found = jnp.where(jnp.logical_and(wanted, piece == i), loc, 0)
        found = jnp.max(found, axis=1, keepdims=True)
        last[8 * i : 8 * i + 8, :] = jnp.broadcast_to(found, (8, 128))
    left = jnp.max(nz + ny, axis=1, keepdims=True)
    flags[gx] = jnp.broadcast_to(left, (8, 128))


def step_kernel(
    owner, fields, incr, flow, mailed, own_codes, unfinished, F, NZ, FL, CT, xs, ye, ys, yr, pool, landing, leaving,
    shelf, tiles, plan, last, flags, plan_s, last_s, lsem, hs, hr, tsend, trecv, fsend, frecv, msem, ssem, rsem, osem,
):
    gx, gy = lax.axis_index("gx"), lax.axis_index("gy")
    edges, flows, block, noise = start_loads(fields, incr, flow, F, NZ, FL, xs, ye, lsem)
    barrier = pltpu.get_barrier_semaphore()
    row_peers = [lax.rem(gy + i, 16) for i in range(1, 16)]
    col_peers = [lax.rem(gx + i, 8) for i in range(1, 8)]
    for peer in row_peers:
        pl.semaphore_signal(barrier, inc=1, device_id=(gx, peer), device_id_type=MESH)
    for peer in col_peers:
        pl.semaphore_signal(barrier, inc=1, device_id=(peer, gy), device_id_type=MESH)
    tiles[gy] = make_tile(owner, gy)
    for copy in edges:
        copy.wait()
    mask_edges(owner, xs, ye, ys)
    pl.semaphore_wait(barrier, 22)
    mail = []
    for i, peer in enumerate(row_peers):
        mail.append(
            pltpu.make_async_remote_copy(
                tiles.at[gy], tiles.at[gy], tsend.at[i], trecv.at[i],
                device_id=(gx, peer), device_id_type=MESH,
            )
        )
    for copy in mail:
        copy.start()
    halos = halo_copies(F, xs, ys, yr, hs, hr)
    for copy in halos:
        copy.start()
    F2 = F.reshape(2, 68 * PITCH, 128)
    for copy in flows:
        copy.wait()
    make_coefficients(FL, CT)
    for copy in block:
        copy.wait()
    mask_block(owner, F2)
    for copy in mail:
        copy.wait()
    plan_routes(tiles, plan, last, flags, gx, gy)
    news = [
        pltpu.make_async_remote_copy(
            flags.at[gx], flags.at[gx], fsend.at[i], frecv.at[i],
            device_id=(peer, gy), device_id_type=MESH,
        )
        for i, peer in enumerate(col_peers)
    ]
    for copy in news:
        copy.start()
    scalars = [
        pltpu.make_async_copy(plan, plan_s, msem.at[0]),
        pltpu.make_async_copy(last, last_s, msem.at[1]),
    ]
    for copy in scalars:
        copy.start()
    for copy in noise:
        copy.wait()
    for copy in halos:
        copy.wait()
    unpack_halo(F2, yr)

    def brick(b):
        row, col = b // 4, lax.rem(b, 4)

        def lines(half, carry):
            for step in range(16):
                coded = brick_line(F2, NZ, CT, row, col, half, step)
                for comp in range(2):
                    place = (PIECES * b + 2 * half + step // 8, pl.ds(32 * (step % 8), 32), pl.ds(128 * comp, 128))
                    pool[place] = coded[comp]
            return carry

        lax.fori_loop(0, 2, lines, 0)

    y, z = gy // 4, lax.rem(gy, 4)
    targets = [
        4 * y + lax.rem(z + 1, 4),
        4 * y + lax.rem(z + 3, 4),
        4 * lax.rem(y + 1, 4) + z,
        4 * lax.rem(y + 3, 4) + z,
    ]

    def hop(r, k):
        side = lax.rem(r, 2)
        return pltpu.make_async_remote_copy(
            leaving.at[side, k], landing.at[r, k], ssem.at[side, k], rsem.at[r, k],
            device_id=(gx, targets[k]), device_id_type=MESH,
        )

    def collect(r):
        for k in range(4):
            copy = hop(r, k)
            copy.wait()
            pool[OWN + 4 * r + k] = landing[r, k]

    def send(r):
        side = lax.rem(r, 2)
        for k in range(4):
            leaving[side, k] = pool[slot_in_pool(plan_s[8 * r, k])]
            hop(r, k).start()

    brick(0)
    for copy in scalars:
        copy.wait()
    send(0)
    brick(1)
    send(1)

    def early(r, carry):
        brick(r)
        collect(r - 2)
        send(r)
        return carry

    lax.fori_loop(2, 8, early, 0)
    keep = pltpu.make_async_copy(pool.at[pl.ds(0, OWN)], own_codes, msem.at[2])
    keep.start()

    def later(r, carry):
        collect(r - 2)
        send(r)
        return carry

    lax.fori_loop(8, ROUNDS, later, 0)
    collect(ROUNDS - 2)
    collect(ROUNDS - 1)

    def deliver(s, carry):
        for i in range(PIECES):
            shelf[PIECES * s + i] = pool[slot_in_pool(last_s[8 * i + s, 0])]
        part = pl.ds(PIECES * s, PIECES)
        pltpu.make_async_copy(shelf.at[part], mailed.at[part], osem.at[s]).start()
        return carry

    lax.fori_loop(0, CAPACITY, deliver, 0)
    for copy in news:
        copy.wait()
    tell = pltpu.make_async_copy(flags, unfinished, msem.at[3])
    tell.start()
    for s in range(CAPACITY):
        part = pl.ds(PIECES * s, PIECES)
        pltpu.make_async_copy(shelf.at[part], mailed.at[part], osem.at[s]).wait()
    keep.wait()
    tell.wait()


def advance(fields, increments, flow_field, brick_owner):
    any_ = pl.BlockSpec(memory_space=pl.ANY)
    packet = (EDGE * EDGE // PIECES, 256)
    dma = pltpu.SemaphoreType.DMA
    return pl.pallas_call(
        step_kernel,
        out_shape=(
            jax.ShapeDtypeStruct((CAPACITY * PIECES, *packet), jnp.int16),
            jax.ShapeDtypeStruct((OWN, *packet), jnp.int16),
            jax.ShapeDtypeStruct((8, 8, 128), jnp.int32),
        ),
        in_specs=[pl.BlockSpec(memory_space=pltpu.SMEM), any_, any_, any_],
        out_specs=(any_, any_, any_),
        scratch_shapes=[
            pltpu.VMEM((2, 68, PITCH, 128), jnp.float32),
            pltpu.VMEM((NX, NY, 256), jnp.bfloat16),
            pltpu.VMEM((6, NX, NY), jnp.float32),
            pltpu.VMEM((4, 128, 128), jnp.float32),
            pltpu.VMEM((2, 2, 2, NY, 128), jnp.float32),
            pltpu.VMEM((2, 2, NX, 8, 128), jnp.float32),
            pltpu.VMEM((2, 2, 2, NX, 128), jnp.float32),
            pltpu.VMEM((2, 2, 2, NX, 128), jnp.float32),
            pltpu.VMEM((OWN + 4 * ROUNDS, *packet), jnp.int16),
            pltpu.VMEM((ROUNDS, 4, *packet), jnp.int16),
            pltpu.VMEM((2, 4, *packet), jnp.int16),
            pltpu.VMEM((CAPACITY * PIECES, *packet), jnp.int16),
            pltpu.VMEM((16, 8, 128), jnp.int32),
            pltpu.VMEM((8 * ROUNDS, 128), jnp.int32),
            pltpu.VMEM((8 * PIECES, 128), jnp.int32),
            pltpu.VMEM((8, 8, 128), jnp.int32),
            pltpu.SMEM((8 * ROUNDS, 128), jnp.int32),
            pltpu.SMEM((8 * PIECES, 128), jnp.int32),
            dma((12,)),
            dma((4,)),
            dma((4,)),
            dma((15,)),
            dma((15,)),
            dma((7,)),
            dma((7,)),
            dma((4,)),
            dma((2, 4)),
            dma((ROUNDS, 4)),
            dma((CAPACITY,)),
        ],
        compiler_params=pltpu.CompilerParams(
            collective_id=0, has_side_effects=True, vmem_limit_bytes=58 * 2**20
        ),
    )(brick_owner, fields, increments, flow_field)


def finish_kernel(source, codes, out):
    out[0] = decode(codes[0]).reshape(out.shape[1:])


def finish(source, arrived, slots):
    return pl.pallas_call(
        finish_kernel,
        out_shape=jax.ShapeDtypeStruct((slots, EDGE, EDGE, 256), jnp.float32),
        grid_spec=pltpu.PrefetchScalarGridSpec(
            num_scalar_prefetch=1,
            grid=(slots, 2),
            in_specs=[pl.BlockSpec((1, 512, 256), lambda s, h, source: (source[s], h, 0))],
            out_specs=pl.BlockSpec((1, 16, EDGE, 256), lambda s, h, source: (s, h, 0, 0)),
        ),
        compiler_params=pltpu.CompilerParams(vmem_limit_bytes=32 * 2**20),
    )(source, arrived)


def pick_kernel(chosen, codes, out):
    out[...] = codes[...]


def pick(chosen, codes, peers):
    block = (1, EDGE * EDGE, 256)
    return pl.pallas_call(
        pick_kernel,
        out_shape=jax.ShapeDtypeStruct((peers, EDGE * EDGE, 256), jnp.int16),
        grid_spec=pltpu.PrefetchScalarGridSpec(
            num_scalar_prefetch=1,
            grid=(peers,),
            in_specs=[pl.BlockSpec(block, lambda s, chosen: (chosen[s], 0, 0))],
            out_specs=pl.BlockSpec(block, lambda s, chosen: (s, 0, 0)),
        ),
        compiler_params=pltpu.CompilerParams(vmem_limit_bytes=32 * 2**20),
    )(chosen, codes)


def dense(codes, owner_table, brick_owner):
    peer_count = lax.axis_size("gy")
    device = lax.axis_index("gx") * peer_count + lax.axis_index("gy")
    owner_flat = brick_owner.reshape(8)
    target = jnp.where(owner_flat >= 0, owner_flat // CAPACITY % peer_count, -1)
    match_grid = target[None, :] == jnp.arange(peer_count, dtype=jnp.int32)[:, None]
    chosen = jnp.sum(jnp.where(match_grid, jnp.arange(8, dtype=jnp.int32)[None, :], 0), axis=1)
    wanted = device * CAPACITY + jnp.arange(CAPACITY, dtype=jnp.int32)
    column = jnp.arange(owner_table.shape[1], dtype=jnp.int32)
    found = owner_table[None, :, :] == wanted[:, None, None]
    source = jnp.sum(jnp.where(found, (column // 4)[None, None, :], 0), axis=(1, 2))
    picked = pick(chosen, codes.reshape(8, EDGE * EDGE, 256), peer_count)
    arrived = lax.all_to_all(picked, "gy", split_axis=0, concat_axis=0, tiled=True)
    return finish(source, arrived, CAPACITY)


def on_device(fields, increments, flow_field, brick_owner):
    mailed, codes, unfinished = advance(fields, increments, flow_field, brick_owner)

    def routed():
        return decode(mailed.reshape(CAPACITY, EDGE, EDGE, 256))

    def fallback():
        owner_table = lax.all_gather(brick_owner, "gy", axis=1, tiled=True)
        return dense(codes, owner_table, brick_owner)

    return lax.cond(jnp.max(unfinished) == 0, routed, fallback)


def solution(mesh):
    in_specs = (P("gx", "gy", None), P("gx", "gy", None), P(None, "gx", "gy"), P("gx", "gy"))
    out_specs = P(("gx", "gy"), None, None, None)
    return jax.shard_map(
        on_device, mesh=mesh, in_specs=in_specs, out_specs=out_specs, check_vma=False
    )
```

```python
import functools
import math

import jax
import jax.numpy as jnp
from jax import lax
from jax.experimental import pallas as pl
from jax.experimental.pallas import tpu as pltpu
from jax.sharding import PartitionSpec as P

MESH = pl.DeviceIdType.MESH
NOISE_SCALE = math.sqrt(0.1)
CODE_MAX = 32767.0
VALUE_MAX = 24.0
EDGE = 32
PITCH = 144
NX, NY = 64, 128
CAPACITY = 7
PIECES = 4
OWN = 8 * PIECES
ROUNDS = 21
DELAY = 2
SEARCH = 2


def encode(value):
    root = jnp.maximum(jnp.abs(value), 1e-30) * (1.0 / VALUE_MAX)
    for _ in range(3):
        root = root * lax.rsqrt(root)
    code = jnp.minimum(root * CODE_MAX + 0.5, CODE_MAX)
    return jnp.where(value < 0.0, -code, code).astype(jnp.int32).astype(jnp.int16)


def decode(code):
    part = code.astype(jnp.float32)
    square = part * (1.0 / CODE_MAX)
    square = square * square
    square = square * square
    square = square * square * VALUE_MAX
    return jnp.where(part < 0.0, -square, square)


def live_of(owner, row, col):
    return jnp.where(owner[row, col] >= 0, 1.0, 0.0).astype(jnp.float32)


def start_loads(fields, incr, flow, F, NZ, FL, xs, ye, lsem):
    copies = []
    k = 0
    edges = []
    for side in range(2):
        for comp in range(2):
            lanes = pl.ds(128 * comp, 128)
            edges.append((fields.at[pl.ds(62 * side, 2), :, lanes], xs.at[side, comp]))
            edges.append((fields.at[:, pl.ds(120 * side, 8), lanes], ye.at[side, comp]))
    for src, dst in edges:
        copies.append(pltpu.make_async_copy(src, dst, lsem.at[k]))
        k += 1
    copies.append(pltpu.make_async_copy(flow, FL, lsem.at[k]))
    k += 1
    for comp in range(2):
        copies.append(
            pltpu.make_async_copy(
                fields.at[:, :, pl.ds(128 * comp, 128)],
                F.at[comp, pl.ds(2, NX), pl.ds(8, NY)],
                lsem.at[k],
            )
        )
        k += 1
    copies.append(pltpu.make_async_copy(incr, NZ, lsem.at[k]))
    for copy in copies:
        copy.start()
    return copies[:8], copies[8:9], copies[9:11], copies[11:]


def mask_edges(owner, xs, ye, ys):
    for side in range(2):
        for comp in range(2):
            for col in range(4):
                part = pl.ds(EDGE * col, EDGE)
                live = live_of(owner, side, col)
                for line in range(2):
                    xs[side, comp, line, part, :] = xs[side, comp, line, part, :] * live
    for side in range(2):
        for row in range(2):
            live = live_of(owner, row, 3 * side)
            for comp in range(2):
                strip = ye.at[side, comp].reshape(NX * 8, 128)
                for line in range(2):
                    for g in range(4):
                        x0 = EDGE * row + 8 * g
                        ys[side, comp, line, pl.ds(x0, 8), :] = (
                            strip[pl.ds(x0 * 8 + 6 * side + line, 8, stride=8), :] * live
                        )


def halo_copies(F, xs, ys, yr, hs, hr):
    gx, gy = lax.axis_index("gx"), lax.axis_index("gy")
    copies = []
    for side in range(2):
        step = 2 * side - 1
        tx = lax.rem(gx + step + 8, 8)
        ty = lax.rem(gy + step + 16, 16)
        copies.append(
            pltpu.make_async_remote_copy(
                xs.at[side],
                F.at[:, pl.ds(66 * (1 - side), 2), pl.ds(8, NY)],
                hs.at[side],
                hr.at[side],
                device_id=(tx, gy),
                device_id_type=MESH,
            )
        )
        copies.append(
            pltpu.make_async_remote_copy(
                ys.at[side],
                yr.at[side],
                hs.at[2 + side],
                hr.at[2 + side],
                device_id=(gx, ty),
                device_id_type=MESH,
            )
        )
    return copies


def make_coefficients(FL, CT):
    u, v = FL[0], FL[1]
    up, un = jnp.maximum(u, 0.0), jnp.minimum(u, 0.0)
    vp, vn = jnp.maximum(v, 0.0), jnp.minimum(v, 0.0)
    keep = 1.0 - 0.15 * ((up - un) + (vp - vn))
    channels = [
        keep + 0.1 * FL[2],
        0.1 * FL[3],
        0.1 * FL[4],
        keep + 0.1 * FL[5],
        0.2 * up,
        -0.2 * un,
        0.2 * vp,
        -0.2 * vn,
    ]
    for g in range(4):
        block = jnp.concatenate([c[16 * g : 16 * g + 16] for c in channels], axis=0)
        CT[g] = block.T


def mask_block(owner, F2):
    for row in range(2):
        for col in range(4):
            live = live_of(owner, row, col)

            def line(x, carry):
                part = pl.ds((2 + EDGE * row + x) * PITCH + 8 + EDGE * col, EDGE)
                for comp in range(2):
                    F2[comp, part, :] = F2[comp, part, :] * live
                return carry

            lax.fori_loop(0, EDGE, line, 0, unroll=2)


def unpack_halo(F2, yr):
    for side in range(2):
        for comp in range(2):
            for line in range(2):
                place = 6 + line if side == 1 else 136 + line
                for g in range(8):
                    F2[comp, pl.ds((2 + 8 * g) * PITCH + place, 8, stride=PITCH), :] = yr[
                        side, comp, line, pl.ds(8 * g, 8), :
                    ]


def brick_line(F2, NZ, CT, row, col, half, step):
    line = EDGE * row + 16 * half + step
    base = (2 + line) * PITCH + 8 + EDGE * col
    ys = pl.ds(pl.multiple_of(EDGE * col, EDGE), EDGE)
    table = CT[2 * row + half, ys, :]
    spots = [16 * k + step for k in range(8)]
    c = [jnp.broadcast_to(table[:, k : k + 1], (EDGE, 128)) for k in spots]
    q = [F2[comp, pl.ds(base, EDGE), :] for comp in range(2)]
    rest = jnp.maximum(20.0 - 0.8 * (q[0] * q[0] + q[1] * q[1]), 2.0)
    soft = pl.reciprocal(rest, approx=True)
    soft = soft * (2.0 - rest * soft)
    out = []
    for comp in range(2):

        def at(shift):
            return F2[comp, pl.ds(base + shift, EDGE), :]

        moved = c[4] * (at(-PITCH) - 0.25 * at(-2 * PITCH))
        moved += c[5] * (at(PITCH) - 0.25 * at(2 * PITCH))
        moved += c[6] * (at(-1) - 0.25 * at(-2))
        moved += c[7] * (at(1) - 0.25 * at(2))
        own, cross = (c[0], c[1]) if comp == 0 else (c[3], c[2])
        noise = NZ[line, ys, pl.ds(128 * comp, 128)].astype(jnp.float32)
        total = (own - soft) * q[comp] + cross * q[1 - comp] + moved + NOISE_SCALE * noise
        out.append(encode(total))
    return out


def slot_in_pool(number):
    return jnp.minimum(jnp.maximum(number, 0), OWN + 4 * ROUNDS - 1)


def make_tile(owner, gy):
    lane = lax.broadcasted_iota(jnp.int32, (8, 128), 1)
    brick = (lane % 32) // PIECES
    tile = jnp.zeros((8, 128), jnp.int32)
    for b in range(8):
        slot = jnp.maximum(owner[b // 4, b % 4], 0)
        code = lax.rem(slot // CAPACITY, 16) * 8 + lax.rem(slot, CAPACITY) + 1
        code = jnp.where(owner[b // 4, b % 4] >= 0, code, 0)
        tile = jnp.where(brick == b, code, tile)
    return jnp.where(lane // 32 == lax.rem(gy, 4), tile, 0)


NZ_, NY_, Z_, Y_, KZ_, KY_, FIRST_, LOC_, READY_ = range(9)
STATE = (8, 512)


def lanes_of():
    p = lax.broadcasted_iota(jnp.int32, STATE, 1)
    return p // 32, (p // PIECES) % 8, p % PIECES


def decode_tiles(tiles):
    code = jnp.concatenate(
        [tiles[4 * q] + tiles[4 * q + 1] + tiles[4 * q + 2] + tiles[4 * q + 3] for q in range(4)], axis=1
    )
    number = jnp.maximum(code - 1, 0)
    return code > 0, number // 8, number % 8


def open_plan(tiles, st):
    src, brick, piece = lanes_of()
    live, dest, _ = decode_tiles(tiles)
    y, z = src // 4, src % 4
    ty, tz = (dest // 4 - y) & 3, (dest % 4 - z) & 3
    tie = (piece + brick + src) & 1
    st[NZ_] = jnp.where(live, jnp.where(tz == 3, 1, tz), 0)
    st[NY_] = jnp.where(live, jnp.where(ty == 3, 1, ty), 0)
    st[Z_] = z
    st[Y_] = y
    st[KZ_] = jnp.where(tz == 2, tie, jnp.where(tz == 3, 1, 0))
    st[KY_] = jnp.where(ty == 2, tie, jnp.where(ty == 3, 1, 0))
    st[FIRST_] = (piece // 2 + brick) & 1
    st[LOC_] = brick * PIECES + piece
    st[READY_] = jnp.maximum(brick - 1, 0)


def balance(st, t):
    nz, ny, z, y = st[NZ_], st[NY_], st[Z_], st[Y_]
    kz, ky, first = st[KZ_], st[KY_], st[FIRST_]
    kind = lax.rem(t, 3)
    one = [jnp.where(kind == i, 1, 0) for i in range(3)]
    flip0 = one[0] * jnp.minimum(nz, 1) * jnp.minimum(ny, 1)
    flip1 = one[1] * (nz >> 1)
    flip2 = one[2] * (ny >> 1)
    row = lax.broadcasted_iota(jnp.int32, STATE, 0)
    other, j = row >> 2, row & 3
    f = first ^ (flip0 * other)
    lz = kz ^ (flip1 * other)
    ly = ky ^ (flip2 * other)
    zfirst = f == 0
    onz = jnp.where(zfirst, jnp.where(j < nz, 1, 0), jnp.where(j >= ny, 1, 0))
    zc = jnp.where(zfirst, jnp.minimum(j, nz), jnp.maximum(j - ny, 0))
    yc = jnp.where(zfirst, jnp.maximum(j - nz, 0), jnp.minimum(j, ny))
    zz = (z + (1 - 2 * lz) * zc) & 3
    yy = (y + (1 - 2 * ly) * yc) & 3
    link = jnp.where(onz == 1, lz, ly + 2) * 16 + yy * 4 + zz
    used = j < nz + ny
    link = jnp.where(used, link, 64)
    rowid = lax.broadcasted_iota(jnp.int32, (64, 512), 0)
    count = jnp.zeros((64, 512), jnp.int32)
    for i in range(4):
        here = jnp.broadcast_to(link[i : i + 1], (64, 512))
        count = count + jnp.where(rowid == here, 1, 0)
    count = count[:, :128] + count[:, 128:256] + count[:, 256:384] + count[:, 384:]
    count = jnp.broadcast_to(jnp.sum(count, axis=1, keepdims=True), (64, 128))
    diagonal = lax.broadcasted_iota(jnp.int32, (64, 128), 0) == lax.broadcasted_iota(jnp.int32, (64, 128), 1)
    count = jnp.where(diagonal, count, 0)
    load = count[0:8]
    for i in range(1, 8):
        load = load + count[8 * i : 8 * i + 8]
    load = jnp.broadcast_to(jnp.sum(load, axis=0, keepdims=True), (8, 128))
    there = jnp.concatenate(
        [jnp.take_along_axis(load, link[:, 128 * q : 128 * q + 128], axis=1) for q in range(4)], axis=1
    )
    shared = one[1] * (1 - onz) + one[2] * onz
    there = there + other * (1 - shared)
    cost = jnp.where(used, there * there, 0) * (2 * other - 1)
    gain = jnp.broadcast_to(jnp.sum(cost, axis=0, keepdims=True), STATE)
    p = lax.broadcasted_iota(jnp.int32, STATE, 1)
    turn = ((p * 7 + (p >> 5) * 3 + t // 3) & 3) == 0
    go = jnp.where(jnp.logical_and(gain < 0, turn), 1, 0)
    st[FIRST_] = first ^ (flip0 * go)
    st[KZ_] = kz ^ (flip1 * go)
    st[KY_] = ky ^ (flip2 * go)


def plan_round(st, plan, r, gy):
    nz, ny, z, y = st[NZ_], st[NY_], st[Z_], st[Y_]
    kz, ky, loc, ready = st[KZ_], st[KY_], st[LOC_], st[READY_]
    rowid = lax.broadcasted_iota(jnp.int32, (64, 512), 0)
    lane = lax.broadcasted_iota(jnp.int32, (8, 128), 1)
    mine = (rowid[:, :1] & 15) == gy
    usez = jnp.logical_and(nz > 0, jnp.logical_or(st[FIRST_] == 0, ny == 0))
    dist = nz + ny
    active = jnp.logical_and(dist > 0, ready <= r)
    k = jnp.where(usez, kz, ky + 2)
    key = jnp.where(active, k * 16 + y * 4 + z, -1)
    score = dist * 512 + loc + 1
    key = jnp.concatenate([key] * 8, axis=0)
    wide = jnp.concatenate([score] * 8, axis=0)
    bids = jnp.where(rowid == key, wide, 0)
    best = jnp.maximum(jnp.max(bids, axis=1, keepdims=True), 1)
    won = jnp.where(bids == best, 1, 0)
    moved = won[0:8]
    for i in range(1, 8):
        moved = jnp.maximum(moved, won[8 * i : 8 * i + 8])
    moved = jnp.broadcast_to(jnp.max(moved, axis=0, keepdims=True), STATE)
    own = jnp.where(mine, best, 0)
    line = jnp.zeros((8, 128), jnp.int32)
    for i in range(4):
        chosen = jnp.max(own[16 * i : 16 * i + 16], axis=0, keepdims=True)
        line = jnp.where(lane == i, jnp.broadcast_to(chosen, (8, 128)), line)
    plan[r] = jnp.maximum(line - 1, 0) & 511
    wentz = jnp.where(usez, moved, 0)
    wenty = moved - wentz
    st[NZ_] = nz - wentz
    st[NY_] = ny - wenty
    st[Z_] = (z + wentz * (1 - 2 * kz)) & 3
    st[Y_] = (y + wenty * (1 - 2 * ky)) & 3
    st[LOC_] = jnp.where(moved == 1, OWN + 4 * r + k, loc)
    st[READY_] = jnp.where(moved == 1, r + 1 + DELAY, ready)


def close_plan(tiles, st, last, flags, gx, gy):
    _, _, piece = lanes_of()
    live, dest, slot = decode_tiles(tiles)
    row = lax.broadcasted_iota(jnp.int32, STATE, 0)
    wanted = jnp.logical_and(live, jnp.logical_and(dest == gy, slot == row))
    for i in range(PIECES):
        found = jnp.where(jnp.logical_and(wanted, piece == i), st[LOC_], 0)
        last[8 * i : 8 * i + 8, :] = jnp.broadcast_to(jnp.max(found, axis=1, keepdims=True), (8, 128))
    left = jnp.max(st[NZ_] + st[NY_], axis=1, keepdims=True)
    flags[gx] = jnp.broadcast_to(left, (8, 128))


def step_kernel(
    owner, fields, incr, flow, mailed, own_codes, unfinished, F, NZ, FL, CT, xs, ye, ys, yr, pool, landing, leaving,
    shelf, tiles, st, plan, last, flags, plan_s, last_s, flags_s,
    lsem, hs, hr, tsend, trecv, fsend, frecv, msem, psem, ssem, rsem, osem,
):
    gx, gy = lax.axis_index("gx"), lax.axis_index("gy")
    edges, flows, block, noise = start_loads(fields, incr, flow, F, NZ, FL, xs, ye, lsem)
    barrier = pltpu.get_barrier_semaphore()
    row_peers = [lax.rem(gy + i, 16) for i in range(1, 16)]
    col_peers = [lax.rem(gx + i, 8) for i in range(1, 8)]
    for peer in row_peers:
        pl.semaphore_signal(barrier, inc=1, device_id=(gx, peer), device_id_type=MESH)
    for peer in col_peers:
        pl.semaphore_signal(barrier, inc=1, device_id=(peer, gy), device_id_type=MESH)
    tiles[gy] = make_tile(owner, gy)
    for copy in edges:
        copy.wait()
    mask_edges(owner, xs, ye, ys)
    pl.semaphore_wait(barrier, 22)
    mail = []
    for i, peer in enumerate(row_peers):
        mail.append(
            pltpu.make_async_remote_copy(
                tiles.at[gy], tiles.at[gy], tsend.at[i], trecv.at[i],
                device_id=(gx, peer), device_id_type=MESH,
            )
        )
    for copy in mail:
        copy.start()
    halos = halo_copies(F, xs, ys, yr, hs, hr)
    for copy in halos:
        copy.start()
    F2 = F.reshape(2, 68 * PITCH, 128)
    for copy in flows:
        copy.wait()
    make_coefficients(FL, CT)
    for copy in block:
        copy.wait()
    mask_block(owner, F2)
    for copy in mail:
        copy.wait()
    open_plan(tiles, st)

    def search(t, carry):
        balance(st, t)
        return carry

    lax.fori_loop(0, 6, search, 0)

    def row_copy(r):
        return pltpu.make_async_copy(plan.at[r], plan_s.at[r], psem.at[r])

    plan_round(st, plan, 0, gy)
    row_copy(0).start()
    for copy in noise:
        copy.wait()
    for copy in halos:
        copy.wait()
    unpack_halo(F2, yr)

    def brick(b):
        row, col = b // 4, lax.rem(b, 4)

        def lines(half, carry):
            for step in range(16):
                coded = brick_line(F2, NZ, CT, row, col, half, step)
                for comp in range(2):
                    place = (PIECES * b + 2 * half + step // 8, pl.ds(32 * (step % 8), 32), pl.ds(128 * comp, 128))
                    pool[place] = coded[comp]
            return carry

        lax.fori_loop(0, 2, lines, 0)

    y, z = gy // 4, lax.rem(gy, 4)
    targets = [
        4 * y + lax.rem(z + 1, 4),
        4 * y + lax.rem(z + 3, 4),
        4 * lax.rem(y + 1, 4) + z,
        4 * lax.rem(y + 3, 4) + z,
    ]

    def hop(r, k):
        side = lax.rem(r, DELAY + 1)
        return pltpu.make_async_remote_copy(
            leaving.at[side, k], landing.at[r, k], ssem.at[side, k], rsem.at[r, k],
            device_id=(gx, targets[k]), device_id_type=MESH,
        )

    def collect(r):
        for k in range(4):
            copy = hop(r, k)
            copy.wait()
            pool[OWN + 4 * r + k] = landing[r, k]

    def send(r):
        side = lax.rem(r, DELAY + 1)
        row_copy(r).wait()
        for k in range(4):
            leaving[side, k] = pool[slot_in_pool(plan_s[r, 0, k])]
            hop(r, k).start()

    def ahead(r):
        for i in range(SEARCH):
            balance(st, SEARCH * r + 6 + i)
        plan_round(st, plan, r + 1, gy)
        row_copy(r + 1).start()

    def opening(b, carry):
        brick(b)
        return carry

    lax.fori_loop(0, 2, opening, 0)

    def early(r, carry):
        @pl.when(r > DELAY)
        def _():
            collect(r - DELAY - 1)

        send(r)
        ahead(r)
        brick(r + 2)
        return carry

    lax.fori_loop(0, 6, early, 0)
    keep = pltpu.make_async_copy(pool.at[pl.ds(0, OWN)], own_codes, msem.at[2])
    keep.start()

    def later(r, carry):
        collect(r - DELAY - 1)
        send(r)
        ahead(r)
        return carry

    lax.fori_loop(6, ROUNDS - 1, later, 0)
    collect(ROUNDS - DELAY - 2)
    send(ROUNDS - 1)
    close_plan(tiles, st, last, flags, gx, gy)
    news = [
        pltpu.make_async_remote_copy(
            flags.at[gx], flags.at[gx], fsend.at[i], frecv.at[i],
            device_id=(peer, gy), device_id_type=MESH,
        )
        for i, peer in enumerate(col_peers)
    ]
    for copy in news:
        copy.start()
    final = pltpu.make_async_copy(last, last_s, msem.at[0])
    final.start()
    for r in range(ROUNDS - DELAY - 1, ROUNDS):
        collect(r)
    final.wait()

    def deliver(s, carry):
        for i in range(PIECES):
            shelf[PIECES * s + i] = pool[slot_in_pool(last_s[8 * i + s, 0])]
        part = pl.ds(PIECES * s, PIECES)
        pltpu.make_async_copy(shelf.at[part], mailed.at[part], osem.at[s]).start()
        return carry

    lax.fori_loop(0, CAPACITY, deliver, 0)
    for copy in news:
        copy.wait()
    tell = pltpu.make_async_copy(flags, flags_s, msem.at[1])
    tell.start()
    for s in range(CAPACITY):
        part = pl.ds(PIECES * s, PIECES)
        pltpu.make_async_copy(shelf.at[part], mailed.at[part], osem.at[s]).wait()
    keep.wait()
    tell.wait()
    left = flags_s[0, 0, 0]
    for g in range(1, 8):
        left = jnp.maximum(left, flags_s[g, 0, 0])
    unfinished[0] = left


def advance(fields, increments, flow_field, brick_owner):
    any_ = pl.BlockSpec(memory_space=pl.ANY)
    packet = (EDGE * EDGE // PIECES, 256)
    dma = pltpu.SemaphoreType.DMA
    return pl.pallas_call(
        step_kernel,
        out_shape=(
            jax.ShapeDtypeStruct((CAPACITY * PIECES, *packet), jnp.int16),
            jax.ShapeDtypeStruct((OWN, *packet), jnp.int16),
            jax.ShapeDtypeStruct((1,), jnp.int32),
        ),
        in_specs=[pl.BlockSpec(memory_space=pltpu.SMEM), any_, any_, any_],
        out_specs=(any_, any_, pl.BlockSpec(memory_space=pltpu.SMEM)),
        scratch_shapes=[
            pltpu.VMEM((2, 68, PITCH, 128), jnp.float32),
            pltpu.VMEM((NX, NY, 256), jnp.bfloat16),
            pltpu.VMEM((6, NX, NY), jnp.float32),
            pltpu.VMEM((4, 128, 128), jnp.float32),
            pltpu.VMEM((2, 2, 2, NY, 128), jnp.float32),
            pltpu.VMEM((2, 2, NX, 8, 128), jnp.float32),
            pltpu.VMEM((2, 2, 2, NX, 128), jnp.float32),
            pltpu.VMEM((2, 2, 2, NX, 128), jnp.float32),
            pltpu.VMEM((OWN + 4 * ROUNDS, *packet), jnp.int16),
            pltpu.VMEM((ROUNDS, 4, *packet), jnp.int16),
            pltpu.VMEM((DELAY + 1, 4, *packet), jnp.int16),
            pltpu.VMEM((CAPACITY * PIECES, *packet), jnp.int16),
            pltpu.VMEM((16, 8, 128), jnp.int32),
            pltpu.VMEM((9, *STATE), jnp.int32),
            pltpu.VMEM((ROUNDS, 8, 128), jnp.int32),
            pltpu.VMEM((8 * PIECES, 128), jnp.int32),
            pltpu.VMEM((8, 8, 128), jnp.int32),
            pltpu.SMEM((ROUNDS, 8, 128), jnp.int32),
            pltpu.SMEM((8 * PIECES, 128), jnp.int32),
            pltpu.SMEM((8, 8, 128), jnp.int32),
            dma((12,)),
            dma((4,)),
            dma((4,)),
            dma((15,)),
            dma((15,)),
            dma((7,)),
            dma((7,)),
            dma((3,)),
            dma((ROUNDS,)),
            dma((DELAY + 1, 4)),
            dma((ROUNDS, 4)),
            dma((CAPACITY,)),
        ],
        compiler_params=pltpu.CompilerParams(
            collective_id=0, has_side_effects=True, vmem_limit_bytes=58 * 2**20
        ),
    )(brick_owner, fields, increments, flow_field)


def finish_kernel(source, codes, out):
    out[0] = decode(codes[0]).reshape(out.shape[1:])


def finish(source, arrived, slots):
    return pl.pallas_call(
        finish_kernel,
        out_shape=jax.ShapeDtypeStruct((slots, EDGE, EDGE, 256), jnp.float32),
        grid_spec=pltpu.PrefetchScalarGridSpec(
            num_scalar_prefetch=1,
            grid=(slots, 2),
            in_specs=[pl.BlockSpec((1, 512, 256), lambda s, h, source: (source[s], h, 0))],
            out_specs=pl.BlockSpec((1, 16, EDGE, 256), lambda s, h, source: (s, h, 0, 0)),
        ),
        compiler_params=pltpu.CompilerParams(vmem_limit_bytes=32 * 2**20),
    )(source, arrived)


def pick_kernel(chosen, codes, out):
    out[...] = codes[...]


def pick(chosen, codes, peers):
    block = (1, EDGE * EDGE, 256)
    return pl.pallas_call(
        pick_kernel,
        out_shape=jax.ShapeDtypeStruct((peers, EDGE * EDGE, 256), jnp.int16),
        grid_spec=pltpu.PrefetchScalarGridSpec(
            num_scalar_prefetch=1,
            grid=(peers,),
            in_specs=[pl.BlockSpec(block, lambda s, chosen: (chosen[s], 0, 0))],
            out_specs=pl.BlockSpec(block, lambda s, chosen: (s, 0, 0)),
        ),
        compiler_params=pltpu.CompilerParams(vmem_limit_bytes=32 * 2**20),
    )(chosen, codes)


def dense(codes, owner_table, brick_owner):
    peer_count = lax.axis_size("gy")
    device = lax.axis_index("gx") * peer_count + lax.axis_index("gy")
    owner_flat = brick_owner.reshape(8)
    target = jnp.where(owner_flat >= 0, owner_flat // CAPACITY % peer_count, -1)
    match_grid = target[None, :] == jnp.arange(peer_count, dtype=jnp.int32)[:, None]
    chosen = jnp.sum(jnp.where(match_grid, jnp.arange(8, dtype=jnp.int32)[None, :], 0), axis=1)
    wanted = device * CAPACITY + jnp.arange(CAPACITY, dtype=jnp.int32)
    column = jnp.arange(owner_table.shape[1], dtype=jnp.int32)
    found = owner_table[None, :, :] == wanted[:, None, None]
    source = jnp.sum(jnp.where(found, (column // 4)[None, None, :], 0), axis=(1, 2))
    picked = pick(chosen, codes.reshape(8, EDGE * EDGE, 256), peer_count)
    arrived = lax.all_to_all(picked, "gy", split_axis=0, concat_axis=0, tiled=True)
    return finish(source, arrived, CAPACITY)


def spread_kernel(codes, out):
    out[...] = decode(codes[...]).reshape(out.shape)


def spread(mailed):
    return pl.pallas_call(
        spread_kernel,
        out_shape=jax.ShapeDtypeStruct((CAPACITY, EDGE, EDGE, 256), jnp.float32),
        grid=(CAPACITY,),
        in_specs=[pl.BlockSpec((PIECES, EDGE * EDGE // PIECES, 256), lambda s: (s, 0, 0))],
        out_specs=pl.BlockSpec((1, EDGE, EDGE, 256), lambda s: (s, 0, 0, 0)),
        compiler_params=pltpu.CompilerParams(vmem_limit_bytes=60 * 2**20),
    )(mailed)


def on_device(fields, increments, flow_field, brick_owner):
    mailed, codes, unfinished = advance(fields, increments, flow_field, brick_owner)

    def routed():
        return spread(mailed)

    def fallback():
        owner_table = lax.all_gather(brick_owner, "gy", axis=1, tiled=True)
        return dense(codes, owner_table, brick_owner)

    return lax.cond(unfinished[0] == 0, routed, fallback)


def solution(mesh):
    in_specs = (P("gx", "gy", None), P("gx", "gy", None), P(None, "gx", "gy"), P("gx", "gy"))
    out_specs = P(("gx", "gy"), None, None, None)
    return jax.shard_map(
        on_device, mesh=mesh, in_specs=in_specs, out_specs=out_specs, check_vma=False
    )
```

```python
import functools
import math

import jax
import jax.numpy as jnp
from jax import lax
from jax.experimental import pallas as pl
from jax.experimental.pallas import tpu as pltpu
from jax.sharding import PartitionSpec as P

MESH = pl.DeviceIdType.MESH
NOISE_SCALE = math.sqrt(0.1)
CODE_MAX = 32767.0
VALUE_MAX = 24.0
EDGE = 32
PITCH = 144
NX, NY = 64, 128
CAPACITY = 7
PIECES = 4
OWN = 8 * PIECES
ROUNDS = 20
DELAY = 2
SEARCH = 2
FIRST_SEARCH = 3


def encode(value):
    root = jnp.maximum(jnp.abs(value), 1e-30) * (1.0 / VALUE_MAX)
    for _ in range(3):
        root = root * lax.rsqrt(root)
    code = jnp.minimum(root * CODE_MAX + 0.5, CODE_MAX)
    return jnp.where(value < 0.0, -code, code).astype(jnp.int32).astype(jnp.int16)


def decode(code):
    part = code.astype(jnp.float32)
    square = part * (1.0 / CODE_MAX)
    square = square * square
    square = square * square
    square = square * square * VALUE_MAX
    return jnp.where(part < 0.0, -square, square)


def live_of(owner, row, col):
    return jnp.where(owner[row, col] >= 0, 1.0, 0.0).astype(jnp.float32)


def start_loads(fields, incr, flow, F, NZ, FL, xs, ye, lsem):
    copies = []
    k = 0
    edges = []
    for side in range(2):
        for comp in range(2):
            lanes = pl.ds(128 * comp, 128)
            edges.append((fields.at[pl.ds(62 * side, 2), :, lanes], xs.at[side, comp]))
            edges.append((fields.at[:, pl.ds(120 * side, 8), lanes], ye.at[side, comp]))
    for src, dst in edges:
        copies.append(pltpu.make_async_copy(src, dst, lsem.at[k]))
        k += 1
    copies.append(pltpu.make_async_copy(flow, FL, lsem.at[k]))
    k += 1
    for comp in range(2):
        copies.append(
            pltpu.make_async_copy(
                fields.at[:, :, pl.ds(128 * comp, 128)],
                F.at[comp, pl.ds(2, NX), pl.ds(8, NY)],
                lsem.at[k],
            )
        )
        k += 1
    copies.append(pltpu.make_async_copy(incr, NZ, lsem.at[k]))
    for copy in copies:
        copy.start()
    return copies[:8], copies[8:9], copies[9:11], copies[11:]


def mask_edges(owner, xs, ye, ys):
    for side in range(2):
        for comp in range(2):
            for col in range(4):
                part = pl.ds(EDGE * col, EDGE)
                live = live_of(owner, side, col)
                for line in range(2):
                    xs[side, comp, line, part, :] = xs[side, comp, line, part, :] * live
    for side in range(2):
        for row in range(2):
            live = live_of(owner, row, 3 * side)
            for comp in range(2):
                strip = ye.at[side, comp].reshape(NX * 8, 128)
                for line in range(2):
                    for g in range(4):
                        x0 = EDGE * row + 8 * g
                        ys[side, comp, line, pl.ds(x0, 8), :] = (
                            strip[pl.ds(x0 * 8 + 6 * side + line, 8, stride=8), :] * live
                        )


def halo_copies(F, xs, ys, yr, hs, hr):
    gx, gy = lax.axis_index("gx"), lax.axis_index("gy")
    copies = []
    for side in range(2):
        step = 2 * side - 1
        tx = lax.rem(gx + step + 8, 8)
        ty = lax.rem(gy + step + 16, 16)
        copies.append(
            pltpu.make_async_remote_copy(
                xs.at[side],
                F.at[:, pl.ds(66 * (1 - side), 2), pl.ds(8, NY)],
                hs.at[side],
                hr.at[side],
                device_id=(tx, gy),
                device_id_type=MESH,
            )
        )
        copies.append(
            pltpu.make_async_remote_copy(
                ys.at[side],
                yr.at[side],
                hs.at[2 + side],
                hr.at[2 + side],
                device_id=(gx, ty),
                device_id_type=MESH,
            )
        )
    return copies


def make_coefficients(FL, CT):
    u, v = FL[0], FL[1]
    up, un = jnp.maximum(u, 0.0), jnp.minimum(u, 0.0)
    vp, vn = jnp.maximum(v, 0.0), jnp.minimum(v, 0.0)
    keep = 1.0 - 0.15 * ((up - un) + (vp - vn))
    channels = [
        keep + 0.1 * FL[2],
        0.1 * FL[3],
        0.1 * FL[4],
        keep + 0.1 * FL[5],
        0.2 * up,
        -0.2 * un,
        0.2 * vp,
        -0.2 * vn,
    ]
    for g in range(4):
        block = jnp.concatenate([c[16 * g : 16 * g + 16] for c in channels], axis=0)
        CT[g] = block.T


def mask_block(owner, F2):
    for row in range(2):
        for col in range(4):
            live = live_of(owner, row, col)

            def line(x, carry):
                part = pl.ds((2 + EDGE * row + x) * PITCH + 8 + EDGE * col, EDGE)
                for comp in range(2):
                    F2[comp, part, :] = F2[comp, part, :] * live
                return carry

            lax.fori_loop(0, EDGE, line, 0, unroll=2)


def unpack_halo(F2, yr):
    for side in range(2):
        for comp in range(2):
            for line in range(2):
                place = 6 + line if side == 1 else 136 + line
                for g in range(8):
                    F2[comp, pl.ds((2 + 8 * g) * PITCH + place, 8, stride=PITCH), :] = yr[
                        side, comp, line, pl.ds(8 * g, 8), :
                    ]


def brick_line(F2, NZ, CT, row, col, half, step):
    line = EDGE * row + 16 * half + step
    base = (2 + line) * PITCH + 8 + EDGE * col
    ys = pl.ds(pl.multiple_of(EDGE * col, EDGE), EDGE)
    table = CT[2 * row + half, ys, :]
    spots = [16 * k + step for k in range(8)]
    c = [jnp.broadcast_to(table[:, k : k + 1], (EDGE, 128)) for k in spots]
    q = [F2[comp, pl.ds(base, EDGE), :] for comp in range(2)]
    rest = jnp.maximum(20.0 - 0.8 * (q[0] * q[0] + q[1] * q[1]), 2.0)
    soft = pl.reciprocal(rest, approx=True)
    soft = soft * (2.0 - rest * soft)
    out = []
    for comp in range(2):

        def at(shift):
            return F2[comp, pl.ds(base + shift, EDGE), :]

        moved = c[4] * (at(-PITCH) - 0.25 * at(-2 * PITCH))
        moved += c[5] * (at(PITCH) - 0.25 * at(2 * PITCH))
        moved += c[6] * (at(-1) - 0.25 * at(-2))
        moved += c[7] * (at(1) - 0.25 * at(2))
        own, cross = (c[0], c[1]) if comp == 0 else (c[3], c[2])
        noise = NZ[line, ys, pl.ds(128 * comp, 128)].astype(jnp.float32)
        total = (own - soft) * q[comp] + cross * q[1 - comp] + moved + NOISE_SCALE * noise
        out.append(encode(total))
    return out


def slot_in_pool(number):
    return jnp.minimum(jnp.maximum(number, 0), OWN + 4 * ROUNDS - 1)


def make_tile(owner, gy):
    lane = lax.broadcasted_iota(jnp.int32, (8, 128), 1)
    brick = (lane % 32) // PIECES
    tile = jnp.zeros((8, 128), jnp.int32)
    for b in range(8):
        slot = jnp.maximum(owner[b // 4, b % 4], 0)
        code = lax.rem(slot // CAPACITY, 16) * 8 + lax.rem(slot, CAPACITY) + 1
        code = jnp.where(owner[b // 4, b % 4] >= 0, code, 0)
        tile = jnp.where(brick == b, code, tile)
    return jnp.where(lane // 32 == lax.rem(gy, 4), tile, 0)


NZ_, NY_, Z_, Y_, KZ_, KY_, FIRST_, LOC_, READY_ = range(9)
STATE = (8, 512)


def lanes_of():
    p = lax.broadcasted_iota(jnp.int32, STATE, 1)
    return p // 32, (p // PIECES) % 8, p % PIECES


def decode_tiles(tiles):
    code = jnp.concatenate(
        [tiles[4 * q] + tiles[4 * q + 1] + tiles[4 * q + 2] + tiles[4 * q + 3] for q in range(4)], axis=1
    )
    number = jnp.maximum(code - 1, 0)
    return code > 0, number // 8, number % 8


def batch_of(brick, piece):
    low, col = brick // 4, brick % 4
    inner = jnp.logical_or(col == 1, col == 2)
    edge = jnp.where(low == 0, jnp.where(piece == 3, 2, 3), jnp.where(piece == 0, 2, 3))
    middle = jnp.where(piece == 1, 0, jnp.where(piece == 2, 1, edge))
    return jnp.where(inner, middle, 4 + piece)


def packet_of(batch, i):
    low, m = i // 2, lax.rem(i, 2)
    brick = jnp.where(batch < 4, 1 + m, 3 * m) + 4 * low
    edge = jnp.where(batch == 2, 3 - 3 * low, 3 * low)
    piece = jnp.where(batch < 2, batch + 1, jnp.where(batch < 4, edge, batch - 4))
    return brick, piece


def open_plan(tiles, st):
    src, brick, piece = lanes_of()
    live, dest, _ = decode_tiles(tiles)
    y, z = src // 4, src % 4
    ty, tz = (dest // 4 - y) & 3, (dest % 4 - z) & 3
    tie = (piece + brick + src) & 1
    st[NZ_] = jnp.where(live, jnp.where(tz == 3, 1, tz), 0)
    st[NY_] = jnp.where(live, jnp.where(ty == 3, 1, ty), 0)
    st[Z_] = z
    st[Y_] = y
    st[KZ_] = jnp.where(tz == 2, tie, jnp.where(tz == 3, 1, 0))
    st[KY_] = jnp.where(ty == 2, tie, jnp.where(ty == 3, 1, 0))
    st[FIRST_] = (piece // 2 + brick) & 1
    st[LOC_] = brick * PIECES + piece
    st[READY_] = jnp.maximum(batch_of(brick, piece) - 1, 0)


def balance(st, t):
    nz, ny, z, y = st[NZ_], st[NY_], st[Z_], st[Y_]
    kz, ky, first = st[KZ_], st[KY_], st[FIRST_]
    kind = lax.rem(t, 3)
    one = [jnp.where(kind == i, 1, 0) for i in range(3)]
    flip0 = one[0] * jnp.minimum(nz, 1) * jnp.minimum(ny, 1)
    flip1 = one[1] * (nz >> 1)
    flip2 = one[2] * (ny >> 1)
    row = lax.broadcasted_iota(jnp.int32, STATE, 0)
    other, j = row >> 2, row & 3
    f = first ^ (flip0 * other)
    lz = kz ^ (flip1 * other)
    ly = ky ^ (flip2 * other)
    zfirst = f == 0
    onz = jnp.where(zfirst, jnp.where(j < nz, 1, 0), jnp.where(j >= ny, 1, 0))
    zc = jnp.where(zfirst, jnp.minimum(j, nz), jnp.maximum(j - ny, 0))
    yc = jnp.where(zfirst, jnp.maximum(j - nz, 0), jnp.minimum(j, ny))
    zz = (z + (1 - 2 * lz) * zc) & 3
    yy = (y + (1 - 2 * ly) * yc) & 3
    link = jnp.where(onz == 1, lz, ly + 2) * 16 + yy * 4 + zz
    used = j < nz + ny
    link = jnp.where(used, link, 64)
    rowid = lax.broadcasted_iota(jnp.int32, (64, 512), 0)
    count = jnp.zeros((64, 512), jnp.int32)
    for i in range(4):
        here = jnp.broadcast_to(link[i : i + 1], (64, 512))
        count = count + jnp.where(rowid == here, 1, 0)
    count = count[:, :128] + count[:, 128:256] + count[:, 256:384] + count[:, 384:]
    count = jnp.broadcast_to(jnp.sum(count, axis=1, keepdims=True), (64, 128))
    diagonal = lax.broadcasted_iota(jnp.int32, (64, 128), 0) == lax.broadcasted_iota(jnp.int32, (64, 128), 1)
    count = jnp.where(diagonal, count, 0)
    load = count[0:8]
    for i in range(1, 8):
        load = load + count[8 * i : 8 * i + 8]
    load = jnp.broadcast_to(jnp.sum(load, axis=0, keepdims=True), (8, 128))
    there = jnp.concatenate(
        [jnp.take_along_axis(load, link[:, 128 * q : 128 * q + 128], axis=1) for q in range(4)], axis=1
    )
    shared = one[1] * (1 - onz) + one[2] * onz
    there = there + other * (1 - shared)
    cost = jnp.where(used, there * there, 0) * (2 * other - 1)
    gain = jnp.broadcast_to(jnp.sum(cost, axis=0, keepdims=True), STATE)
    p = lax.broadcasted_iota(jnp.int32, STATE, 1)
    turn = ((p * 7 + (p >> 5) * 3 + t // 3) & 3) == 0
    go = jnp.where(jnp.logical_and(gain < 0, turn), 1, 0)
    st[FIRST_] = first ^ (flip0 * go)
    st[KZ_] = kz ^ (flip1 * go)
    st[KY_] = ky ^ (flip2 * go)


def plan_round(st, plan, r, gy):
    nz, ny, z, y = st[NZ_], st[NY_], st[Z_], st[Y_]
    kz, ky, loc, ready = st[KZ_], st[KY_], st[LOC_], st[READY_]
    rowid = lax.broadcasted_iota(jnp.int32, (64, 512), 0)
    lane = lax.broadcasted_iota(jnp.int32, (8, 128), 1)
    mine = (rowid[:, :1] & 15) == gy
    usez = jnp.logical_and(nz > 0, jnp.logical_or(st[FIRST_] == 0, ny == 0))
    dist = nz + ny
    active = jnp.logical_and(dist > 0, ready <= r)
    k = jnp.where(usez, kz, ky + 2)
    key = jnp.where(active, k * 16 + y * 4 + z, -1)
    score = dist * 512 + loc + 1
    key = jnp.concatenate([key] * 8, axis=0)
    wide = jnp.concatenate([score] * 8, axis=0)
    bids = jnp.where(rowid == key, wide, 0)
    best = jnp.maximum(jnp.max(bids, axis=1, keepdims=True), 1)
    won = jnp.where(bids == best, 1, 0)
    moved = won[0:8]
    for i in range(1, 8):
        moved = jnp.maximum(moved, won[8 * i : 8 * i + 8])
    moved = jnp.broadcast_to(jnp.max(moved, axis=0, keepdims=True), STATE)
    own = jnp.where(mine, best, 0)
    line = jnp.zeros((8, 128), jnp.int32)
    for i in range(4):
        chosen = jnp.max(own[16 * i : 16 * i + 16], axis=0, keepdims=True)
        line = jnp.where(lane == i, jnp.broadcast_to(chosen, (8, 128)), line)
    plan[r] = jnp.maximum(line - 1, 0) & 511
    wentz = jnp.where(usez, moved, 0)
    wenty = moved - wentz
    st[NZ_] = nz - wentz
    st[NY_] = ny - wenty
    st[Z_] = (z + wentz * (1 - 2 * kz)) & 3
    st[Y_] = (y + wenty * (1 - 2 * ky)) & 3
    st[LOC_] = jnp.where(moved == 1, OWN + 4 * r + k, loc)
    st[READY_] = jnp.where(moved == 1, r + 1 + DELAY, ready)


def close_plan(tiles, st, last, flags, gx, gy):
    _, _, piece = lanes_of()
    live, dest, slot = decode_tiles(tiles)
    row = lax.broadcasted_iota(jnp.int32, STATE, 0)
    wanted = jnp.logical_and(live, jnp.logical_and(dest == gy, slot == row))
    for i in range(PIECES):
        found = jnp.where(jnp.logical_and(wanted, piece == i), st[LOC_], 0)
        last[8 * i : 8 * i + 8, :] = jnp.broadcast_to(jnp.max(found, axis=1, keepdims=True), (8, 128))
    left = jnp.max(st[NZ_] + st[NY_], axis=1, keepdims=True)
    flags[gx] = jnp.broadcast_to(left, (8, 128))


def step_kernel(
    owner, fields, incr, flow, mailed, own_codes, unfinished, F, NZ, FL, CT, xs, ye, ys, yr, pool, landing, leaving,
    shelf, tiles, st, plan, last, flags, plan_s, last_s, flags_s,
    lsem, hs, hr, tsend, trecv, fsend, frecv, msem, psem, ssem, rsem, osem,
):
    gx, gy = lax.axis_index("gx"), lax.axis_index("gy")
    edges, flows, block, noise = start_loads(fields, incr, flow, F, NZ, FL, xs, ye, lsem)
    barrier = pltpu.get_barrier_semaphore()
    row_peers = [lax.rem(gy + i, 16) for i in range(1, 16)]
    col_peers = [lax.rem(gx + i, 8) for i in range(1, 8)]
    for peer in row_peers:
        pl.semaphore_signal(barrier, inc=1, device_id=(gx, peer), device_id_type=MESH)
    for peer in col_peers:
        pl.semaphore_signal(barrier, inc=1, device_id=(peer, gy), device_id_type=MESH)
    tiles[gy] = make_tile(owner, gy)
    pl.semaphore_wait(barrier, 22)
    mail = []
    for i, peer in enumerate(row_peers):
        mail.append(
            pltpu.make_async_remote_copy(
                tiles.at[gy], tiles.at[gy], tsend.at[i], trecv.at[i],
                device_id=(gx, peer), device_id_type=MESH,
            )
        )
    for copy in mail:
        copy.start()
    for copy in edges:
        copy.wait()
    mask_edges(owner, xs, ye, ys)
    halos = halo_copies(F, xs, ys, yr, hs, hr)
    for copy in halos:
        copy.start()
    F2 = F.reshape(2, 68 * PITCH, 128)
    for copy in flows:
        copy.wait()
    make_coefficients(FL, CT)
    for copy in block:
        copy.wait()
    mask_block(owner, F2)
    for copy in noise:
        copy.wait()

    def compute(batch):
        def packet(i, carry):
            b, piece = packet_of(batch, i)
            row, col = b // 4, lax.rem(b, 4)
            for odd in range(2):

                @pl.when(lax.rem(piece, 2) == odd)
                def _():
                    for step in range(8):
                        coded = brick_line(F2, NZ, CT, row, col, piece // 2, 8 * odd + step)
                        for comp in range(2):
                            pool[PIECES * b + piece, pl.ds(32 * step, 32), pl.ds(128 * comp, 128)] = coded[comp]

            return carry

        lax.fori_loop(0, 4, packet, 0)

    y, z = gy // 4, lax.rem(gy, 4)
    targets = [
        4 * y + lax.rem(z + 1, 4),
        4 * y + lax.rem(z + 3, 4),
        4 * lax.rem(y + 1, 4) + z,
        4 * lax.rem(y + 3, 4) + z,
    ]

    def row_copy(r):
        return pltpu.make_async_copy(plan.at[r], plan_s.at[r], psem.at[r])

    def hop(r, k):
        side = lax.rem(r, DELAY + 1)
        return pltpu.make_async_remote_copy(
            leaving.at[side, k], landing.at[r, k], ssem.at[side, k], rsem.at[r, k],
            device_id=(gx, targets[k]), device_id_type=MESH,
        )

    def collect(r):
        for k in range(4):
            copy = hop(r, k)
            copy.wait()
            pool[OWN + 4 * r + k] = landing[r, k]

    def send(r):
        side = lax.rem(r, DELAY + 1)
        row_copy(r).wait()
        for k in range(4):
            leaving[side, k] = pool[slot_in_pool(plan_s[r, 0, k])]
            hop(r, k).start()

    def ahead(r, steps):
        for i in range(steps):
            balance(st, 3 * r + FIRST_SEARCH + i)
        plan_round(st, plan, r + 1, gy)
        row_copy(r + 1).start()

    def search(t, carry):
        balance(st, t)
        return carry

    def opening(j, carry):
        compute(j)

        @pl.when(j == 0)
        def _():
            for copy in mail:
                copy.wait()
            open_plan(tiles, st)
            lax.fori_loop(0, FIRST_SEARCH, search, 0)
            plan_round(st, plan, 0, gy)
            row_copy(0).start()

        return carry

    lax.fori_loop(0, 2, opening, 0)

    def early(r, carry):
        @pl.when(r > DELAY)
        def _():
            collect(r - DELAY - 1)

        send(r)
        ahead(r, SEARCH)
        compute(r + 2)

        @pl.when(r == 0)
        def _():
            for copy in halos:
                copy.wait()
            unpack_halo(F2, yr)

        return carry

    lax.fori_loop(0, 6, early, 0)
    keep = pltpu.make_async_copy(pool.at[pl.ds(0, OWN)], own_codes, msem.at[2])
    keep.start()

    def later(r, carry):
        collect(r - DELAY - 1)
        send(r)
        ahead(r, 3)
        return carry

    lax.fori_loop(6, ROUNDS - 1, later, 0)
    collect(ROUNDS - DELAY - 2)
    send(ROUNDS - 1)
    close_plan(tiles, st, last, flags, gx, gy)
    news = [
        pltpu.make_async_remote_copy(
            flags.at[gx], flags.at[gx], fsend.at[i], frecv.at[i],
            device_id=(peer, gy), device_id_type=MESH,
        )
        for i, peer in enumerate(col_peers)
    ]
    for copy in news:
        copy.start()
    final = pltpu.make_async_copy(last, last_s, msem.at[0])
    final.start()
    for r in range(ROUNDS - DELAY - 1, ROUNDS):
        collect(r)
    final.wait()

    def deliver(s, carry):
        for i in range(PIECES):
            shelf[PIECES * s + i] = pool[slot_in_pool(last_s[8 * i + s, 0])]
        part = pl.ds(PIECES * s, PIECES)
        pltpu.make_async_copy(shelf.at[part], mailed.at[part], osem.at[s]).start()
        return carry

    lax.fori_loop(0, CAPACITY, deliver, 0)
    for copy in news:
        copy.wait()
    tell = pltpu.make_async_copy(flags, flags_s, msem.at[1])
    tell.start()
    for s in range(CAPACITY):
        part = pl.ds(PIECES * s, PIECES)
        pltpu.make_async_copy(shelf.at[part], mailed.at[part], osem.at[s]).wait()
    keep.wait()
    tell.wait()
    left = flags_s[0, 0, 0]
    for g in range(1, 8):
        left = jnp.maximum(left, flags_s[g, 0, 0])
    unfinished[0] = left


def advance(fields, increments, flow_field, brick_owner):
    any_ = pl.BlockSpec(memory_space=pl.ANY)
    packet = (EDGE * EDGE // PIECES, 256)
    dma = pltpu.SemaphoreType.DMA
    return pl.pallas_call(
        step_kernel,
        out_shape=(
            jax.ShapeDtypeStruct((CAPACITY * PIECES, *packet), jnp.int16),
            jax.ShapeDtypeStruct((OWN, *packet), jnp.int16),
            jax.ShapeDtypeStruct((1,), jnp.int32),
        ),
        in_specs=[pl.BlockSpec(memory_space=pltpu.SMEM), any_, any_, any_],
        out_specs=(any_, any_, pl.BlockSpec(memory_space=pltpu.SMEM)),
        scratch_shapes=[
            pltpu.VMEM((2, 68, PITCH, 128), jnp.float32),
            pltpu.VMEM((NX, NY, 256), jnp.bfloat16),
            pltpu.VMEM((6, NX, NY), jnp.float32),
            pltpu.VMEM((4, 128, 128), jnp.float32),
            pltpu.VMEM((2, 2, 2, NY, 128), jnp.float32),
            pltpu.VMEM((2, 2, NX, 8, 128), jnp.float32),
            pltpu.VMEM((2, 2, 2, NX, 128), jnp.float32),
            pltpu.VMEM((2, 2, 2, NX, 128), jnp.float32),
            pltpu.VMEM((OWN + 4 * ROUNDS, *packet), jnp.int16),
            pltpu.VMEM((ROUNDS, 4, *packet), jnp.int16),
            pltpu.VMEM((DELAY + 1, 4, *packet), jnp.int16),
            pltpu.VMEM((CAPACITY * PIECES, *packet), jnp.int16),
            pltpu.VMEM((16, 8, 128), jnp.int32),
            pltpu.VMEM((9, *STATE), jnp.int32),
            pltpu.VMEM((ROUNDS, 8, 128), jnp.int32),
            pltpu.VMEM((8 * PIECES, 128), jnp.int32),
            pltpu.VMEM((8, 8, 128), jnp.int32),
            pltpu.SMEM((ROUNDS, 8, 128), jnp.int32),
            pltpu.SMEM((8 * PIECES, 128), jnp.int32),
            pltpu.SMEM((8, 8, 128), jnp.int32),
            dma((12,)),
            dma((4,)),
            dma((4,)),
            dma((15,)),
            dma((15,)),
            dma((7,)),
            dma((7,)),
            dma((3,)),
            dma((ROUNDS,)),
            dma((DELAY + 1, 4)),
            dma((ROUNDS, 4)),
            dma((CAPACITY,)),
        ],
        compiler_params=pltpu.CompilerParams(
            collective_id=0, has_side_effects=True, vmem_limit_bytes=58 * 2**20
        ),
    )(brick_owner, fields, increments, flow_field)


def finish_kernel(source, codes, out):
    out[0] = decode(codes[0]).reshape(out.shape[1:])


def finish(source, arrived, slots):
    return pl.pallas_call(
        finish_kernel,
        out_shape=jax.ShapeDtypeStruct((slots, EDGE, EDGE, 256), jnp.float32),
        grid_spec=pltpu.PrefetchScalarGridSpec(
            num_scalar_prefetch=1,
            grid=(slots, 2),
            in_specs=[pl.BlockSpec((1, 512, 256), lambda s, h, source: (source[s], h, 0))],
            out_specs=pl.BlockSpec((1, 16, EDGE, 256), lambda s, h, source: (s, h, 0, 0)),
        ),
        compiler_params=pltpu.CompilerParams(vmem_limit_bytes=32 * 2**20),
    )(source, arrived)


def pick_kernel(chosen, codes, out):
    out[...] = codes[...]


def pick(chosen, codes, peers):
    block = (1, EDGE * EDGE, 256)
    return pl.pallas_call(
        pick_kernel,
        out_shape=jax.ShapeDtypeStruct((peers, EDGE * EDGE, 256), jnp.int16),
        grid_spec=pltpu.PrefetchScalarGridSpec(
            num_scalar_prefetch=1,
            grid=(peers,),
            in_specs=[pl.BlockSpec(block, lambda s, chosen: (chosen[s], 0, 0))],
            out_specs=pl.BlockSpec(block, lambda s, chosen: (s, 0, 0)),
        ),
        compiler_params=pltpu.CompilerParams(vmem_limit_bytes=32 * 2**20),
    )(chosen, codes)


def dense(codes, owner_table, brick_owner):
    peer_count = lax.axis_size("gy")
    device = lax.axis_index("gx") * peer_count + lax.axis_index("gy")
    owner_flat = brick_owner.reshape(8)
    target = jnp.where(owner_flat >= 0, owner_flat // CAPACITY % peer_count, -1)
    match_grid = target[None, :] == jnp.arange(peer_count, dtype=jnp.int32)[:, None]
    chosen = jnp.sum(jnp.where(match_grid, jnp.arange(8, dtype=jnp.int32)[None, :], 0), axis=1)
    wanted = device * CAPACITY + jnp.arange(CAPACITY, dtype=jnp.int32)
    column = jnp.arange(owner_table.shape[1], dtype=jnp.int32)
    found = owner_table[None, :, :] == wanted[:, None, None]
    source = jnp.sum(jnp.where(found, (column // 4)[None, None, :], 0), axis=(1, 2))
    picked = pick(chosen, codes.reshape(8, EDGE * EDGE, 256), peer_count)
    arrived = lax.all_to_all(picked, "gy", split_axis=0, concat_axis=0, tiled=True)
    return finish(source, arrived, CAPACITY)


def spread_kernel(codes, out, taken, made, isem, osem):
    packets = CAPACITY * PIECES

    def arrive(i):
        return pltpu.make_async_copy(codes.at[pl.ds(2 * i, 2)], taken.at[pl.ds(2 * i, 2)], isem.at[i])

    def leave(i):
        return pltpu.make_async_copy(made.at[i], out.at[i // 2, pl.ds(16 * lax.rem(i, 2), 16)], osem.at[i])

    for i in range(packets // 2):
        arrive(i).start()

    def half(i, carry):
        arrive(i).wait()
        for j in range(2):
            made[i, pl.ds(8 * j, 8)] = decode(taken[2 * i + j]).reshape(8, EDGE, 256)
        leave(i).start()
        return carry

    lax.fori_loop(0, packets // 2, half, 0)
    for i in range(packets // 2):
        leave(i).wait()


def spread(mailed):
    packets = CAPACITY * PIECES
    return pl.pallas_call(
        spread_kernel,
        out_shape=jax.ShapeDtypeStruct((CAPACITY, EDGE, EDGE, 256), jnp.float32),
        in_specs=[pl.BlockSpec(memory_space=pl.ANY)],
        out_specs=pl.BlockSpec(memory_space=pl.ANY),
        scratch_shapes=[
            pltpu.VMEM((packets, EDGE * EDGE // PIECES, 256), jnp.int16),
            pltpu.VMEM((packets // 2, 16, EDGE, 256), jnp.float32),
            pltpu.SemaphoreType.DMA((packets // 2,)),
            pltpu.SemaphoreType.DMA((packets // 2,)),
        ],
        compiler_params=pltpu.CompilerParams(vmem_limit_bytes=60 * 2**20),
    )(mailed)


def on_device(fields, increments, flow_field, brick_owner):
    mailed, codes, unfinished = advance(fields, increments, flow_field, brick_owner)

    def routed():
        return spread(mailed)

    def fallback():
        owner_table = lax.all_gather(brick_owner, "gy", axis=1, tiled=True)
        return dense(codes, owner_table, brick_owner)

    return lax.cond(unfinished[0] == 0, routed, fallback)


def solution(mesh):
    in_specs = (P("gx", "gy", None), P("gx", "gy", None), P(None, "gx", "gy"), P("gx", "gy"))
    out_specs = P(("gx", "gy"), None, None, None)
    return jax.shard_map(
        on_device, mesh=mesh, in_specs=in_specs, out_specs=out_specs, check_vma=False
    )
```

```python
import functools
import math

import jax
import jax.numpy as jnp
from jax import lax
from jax.experimental import pallas as pl
from jax.experimental.pallas import tpu as pltpu
from jax.sharding import PartitionSpec as P

MESH = pl.DeviceIdType.MESH
NOISE_SCALE = math.sqrt(0.1)
CODE_MAX = 32767.0
VALUE_MAX = 24.0
EDGE = 32
PITCH = 144
NX, NY = 64, 128
CAPACITY = 7
PIECES = 4
OWN = 8 * PIECES
ROUNDS = 20
DELAY = 2
SEARCH = 1
FIRST_SEARCH = 3


def encode(value):
    root = jnp.maximum(jnp.abs(value), 1e-30) * (1.0 / VALUE_MAX)
    for _ in range(3):
        root = root * lax.rsqrt(root)
    code = jnp.minimum(root * CODE_MAX + 0.5, CODE_MAX)
    return jnp.where(value < 0.0, -code, code).astype(jnp.int32).astype(jnp.int16)


def decode(code):
    part = code.astype(jnp.float32)
    square = part * (1.0 / CODE_MAX)
    square = square * square
    square = square * square
    square = square * square * VALUE_MAX
    return jnp.where(part < 0.0, -square, square)


def live_of(owner, row, col):
    return jnp.where(owner[row, col] >= 0, 1.0, 0.0).astype(jnp.float32)


def start_loads(fields, incr, flow, F, NZ, FL, xs, ye, lsem):
    copies = []
    k = 0
    edges = []
    for side in range(2):
        for comp in range(2):
            lanes = pl.ds(128 * comp, 128)
            edges.append((fields.at[pl.ds(62 * side, 2), :, lanes], xs.at[side, comp]))
            edges.append((fields.at[:, pl.ds(120 * side, 8), lanes], ye.at[side, comp]))
    for src, dst in edges:
        copies.append(pltpu.make_async_copy(src, dst, lsem.at[k]))
        k += 1
    copies.append(pltpu.make_async_copy(flow, FL, lsem.at[k]))
    k += 1
    for comp in range(2):
        copies.append(
            pltpu.make_async_copy(
                fields.at[:, :, pl.ds(128 * comp, 128)],
                F.at[comp, pl.ds(2, NX), pl.ds(8, NY)],
                lsem.at[k],
            )
        )
        k += 1
    copies.append(pltpu.make_async_copy(incr, NZ, lsem.at[k]))
    for copy in copies:
        copy.start()
    return copies[:8], copies[8:9], copies[9:11], copies[11:]


def mask_edges(owner, xs, ye, ys):
    for side in range(2):
        for comp in range(2):
            for col in range(4):
                part = pl.ds(EDGE * col, EDGE)
                live = live_of(owner, side, col)
                for line in range(2):
                    xs[side, comp, line, part, :] = xs[side, comp, line, part, :] * live
    for side in range(2):
        for row in range(2):
            live = live_of(owner, row, 3 * side)
            for comp in range(2):
                strip = ye.at[side, comp].reshape(NX * 8, 128)
                for line in range(2):
                    for g in range(4):
                        x0 = EDGE * row + 8 * g
                        ys[side, comp, line, pl.ds(x0, 8), :] = (
                            strip[pl.ds(x0 * 8 + 6 * side + line, 8, stride=8), :] * live
                        )


def halo_copies(F, xs, ys, yr, hs, hr):
    gx, gy = lax.axis_index("gx"), lax.axis_index("gy")
    copies = []
    for side in range(2):
        step = 2 * side - 1
        tx = lax.rem(gx + step + 8, 8)
        ty = lax.rem(gy + step + 16, 16)
        copies.append(
            pltpu.make_async_remote_copy(
                xs.at[side],
                F.at[:, pl.ds(66 * (1 - side), 2), pl.ds(8, NY)],
                hs.at[side],
                hr.at[side],
                device_id=(tx, gy),
                device_id_type=MESH,
            )
        )
        copies.append(
            pltpu.make_async_remote_copy(
                ys.at[side],
                yr.at[side],
                hs.at[2 + side],
                hr.at[2 + side],
                device_id=(gx, ty),
                device_id_type=MESH,
            )
        )
    return copies


def make_coefficients(FL, CT):
    u, v = FL[0], FL[1]
    up, un = jnp.maximum(u, 0.0), jnp.minimum(u, 0.0)
    vp, vn = jnp.maximum(v, 0.0), jnp.minimum(v, 0.0)
    keep = 1.0 - 0.15 * ((up - un) + (vp - vn))
    channels = [
        keep + 0.1 * FL[2],
        0.1 * FL[3],
        0.1 * FL[4],
        keep + 0.1 * FL[5],
        0.2 * up,
        -0.2 * un,
        0.2 * vp,
        -0.2 * vn,
    ]
    for g in range(4):
        block = jnp.concatenate([c[16 * g : 16 * g + 16] for c in channels], axis=0)
        CT[g] = block.T


def mask_block(owner, F2):
    for row in range(2):
        for col in range(4):
            live = live_of(owner, row, col)

            def line(x, carry):
                part = pl.ds((2 + EDGE * row + x) * PITCH + 8 + EDGE * col, EDGE)
                for comp in range(2):
                    F2[comp, part, :] = F2[comp, part, :] * live
                return carry

            lax.fori_loop(0, EDGE, line, 0, unroll=2)


def unpack_halo(F2, yr):
    for side in range(2):
        for comp in range(2):
            for line in range(2):
                place = 6 + line if side == 1 else 136 + line
                for g in range(8):
                    F2[comp, pl.ds((2 + 8 * g) * PITCH + place, 8, stride=PITCH), :] = yr[
                        side, comp, line, pl.ds(8 * g, 8), :
                    ]


def brick_line(F2, NZ, CT, row, col, half, step):
    line = EDGE * row + 16 * half + step
    base = (2 + line) * PITCH + 8 + EDGE * col
    ys = pl.ds(pl.multiple_of(EDGE * col, EDGE), EDGE)
    table = CT[2 * row + half, ys, :]
    spots = [16 * k + step for k in range(8)]
    c = [jnp.broadcast_to(table[:, k : k + 1], (EDGE, 128)) for k in spots]
    q = [F2[comp, pl.ds(base, EDGE), :] for comp in range(2)]
    rest = jnp.maximum(20.0 - 0.8 * (q[0] * q[0] + q[1] * q[1]), 2.0)
    soft = pl.reciprocal(rest, approx=True)
    soft = soft * (2.0 - rest * soft)
    out = []
    for comp in range(2):

        def at(shift):
            return F2[comp, pl.ds(base + shift, EDGE), :]

        moved = c[4] * (at(-PITCH) - 0.25 * at(-2 * PITCH))
        moved += c[5] * (at(PITCH) - 0.25 * at(2 * PITCH))
        moved += c[6] * (at(-1) - 0.25 * at(-2))
        moved += c[7] * (at(1) - 0.25 * at(2))
        own, cross = (c[0], c[1]) if comp == 0 else (c[3], c[2])
        noise = NZ[line, ys, pl.ds(128 * comp, 128)].astype(jnp.float32)
        total = (own - soft) * q[comp] + cross * q[1 - comp] + moved + NOISE_SCALE * noise
        out.append(encode(total))
    return out


def slot_in_pool(number):
    return jnp.minimum(jnp.maximum(number, 0), OWN + 4 * ROUNDS - 1)


def make_tile(owner, gy):
    lane = lax.broadcasted_iota(jnp.int32, (8, 128), 1)
    brick = (lane % 32) // PIECES
    tile = jnp.zeros((8, 128), jnp.int32)
    for b in range(8):
        slot = jnp.maximum(owner[b // 4, b % 4], 0)
        code = lax.rem(slot // CAPACITY, 16) * 8 + lax.rem(slot, CAPACITY) + 1
        code = jnp.where(owner[b // 4, b % 4] >= 0, code, 0)
        tile = jnp.where(brick == b, code, tile)
    return jnp.where(lane // 32 == lax.rem(gy, 4), tile, 0)


NZ_, NY_, Z_, Y_, KZ_, KY_, FIRST_, LOC_, READY_ = range(9)
STATE = (8, 512)


def lanes_of():
    p = lax.broadcasted_iota(jnp.int32, STATE, 1)
    return p // 32, (p // PIECES) % 8, p % PIECES


def decode_tiles(tiles):
    code = jnp.concatenate(
        [tiles[4 * q] + tiles[4 * q + 1] + tiles[4 * q + 2] + tiles[4 * q + 3] for q in range(4)], axis=1
    )
    number = jnp.maximum(code - 1, 0)
    return code > 0, number // 8, number % 8


def batch_of(brick, piece):
    low, col = brick // 4, brick % 4
    inner = jnp.logical_or(col == 1, col == 2)
    edge = jnp.where(low == 0, jnp.where(piece == 3, 2, 3), jnp.where(piece == 0, 2, 3))
    middle = jnp.where(piece == 1, 0, jnp.where(piece == 2, 1, edge))
    return jnp.where(inner, middle, 4 + piece)


def packet_of(batch, i):
    low, m = i // 2, lax.rem(i, 2)
    brick = jnp.where(batch < 4, 1 + m, 3 * m) + 4 * low
    edge = jnp.where(batch == 2, 3 - 3 * low, 3 * low)
    piece = jnp.where(batch < 2, batch + 1, jnp.where(batch < 4, edge, batch - 4))
    return brick, piece


def open_plan(tiles, st):
    src, brick, piece = lanes_of()
    live, dest, _ = decode_tiles(tiles)
    y, z = src // 4, src % 4
    ty, tz = (dest // 4 - y) & 3, (dest % 4 - z) & 3
    tie = (piece + brick + src) & 1
    st[NZ_] = jnp.where(live, jnp.where(tz == 3, 1, tz), 0)
    st[NY_] = jnp.where(live, jnp.where(ty == 3, 1, ty), 0)
    st[Z_] = z
    st[Y_] = y
    st[KZ_] = jnp.where(tz == 2, tie, jnp.where(tz == 3, 1, 0))
    st[KY_] = jnp.where(ty == 2, tie, jnp.where(ty == 3, 1, 0))
    st[FIRST_] = (piece // 2 + brick) & 1
    st[LOC_] = brick * PIECES + piece
    st[READY_] = jnp.maximum(batch_of(brick, piece) - 1, 0)


def balance(st, t):
    nz, ny, z, y = st[NZ_], st[NY_], st[Z_], st[Y_]
    kz, ky, first = st[KZ_], st[KY_], st[FIRST_]
    kind = lax.rem(t, 3)
    one = [jnp.where(kind == i, 1, 0) for i in range(3)]
    flip0 = one[0] * jnp.minimum(nz, 1) * jnp.minimum(ny, 1)
    flip1 = one[1] * (nz >> 1)
    flip2 = one[2] * (ny >> 1)
    row = lax.broadcasted_iota(jnp.int32, STATE, 0)
    other, j = row >> 2, row & 3
    f = first ^ (flip0 * other)
    lz = kz ^ (flip1 * other)
    ly = ky ^ (flip2 * other)
    zfirst = f == 0
    onz = jnp.where(zfirst, jnp.where(j < nz, 1, 0), jnp.where(j >= ny, 1, 0))
    zc = jnp.where(zfirst, jnp.minimum(j, nz), jnp.maximum(j - ny, 0))
    yc = jnp.where(zfirst, jnp.maximum(j - nz, 0), jnp.minimum(j, ny))
    zz = (z + (1 - 2 * lz) * zc) & 3
    yy = (y + (1 - 2 * ly) * yc) & 3
    link = jnp.where(onz == 1, lz, ly + 2) * 16 + yy * 4 + zz
    used = j < nz + ny
    link = jnp.where(used, link, 64)
    rowid = lax.broadcasted_iota(jnp.int32, (64, 512), 0)
    count = jnp.zeros((64, 512), jnp.int32)
    for i in range(4):
        here = jnp.broadcast_to(link[i : i + 1], (64, 512))
        count = count + jnp.where(rowid == here, 1, 0)
    count = count[:, :128] + count[:, 128:256] + count[:, 256:384] + count[:, 384:]
    count = jnp.broadcast_to(jnp.sum(count, axis=1, keepdims=True), (64, 128))
    diagonal = lax.broadcasted_iota(jnp.int32, (64, 128), 0) == lax.broadcasted_iota(jnp.int32, (64, 128), 1)
    count = jnp.where(diagonal, count, 0)
    load = count[0:8]
    for i in range(1, 8):
        load = load + count[8 * i : 8 * i + 8]
    load = jnp.broadcast_to(jnp.sum(load, axis=0, keepdims=True), (8, 128))
    there = jnp.concatenate(
        [jnp.take_along_axis(load, link[:, 128 * q : 128 * q + 128], axis=1) for q in range(4)], axis=1
    )
    shared = one[1] * (1 - onz) + one[2] * onz
    there = there + other * (1 - shared)
    cost = jnp.where(used, there * there, 0) * (2 * other - 1)
    gain = jnp.broadcast_to(jnp.sum(cost, axis=0, keepdims=True), STATE)
    p = lax.broadcasted_iota(jnp.int32, STATE, 1)
    turn = ((p * 7 + (p >> 5) * 3 + t // 3) & 3) == 0
    go = jnp.where(jnp.logical_and(gain < 0, turn), 1, 0)
    st[FIRST_] = first ^ (flip0 * go)
    st[KZ_] = kz ^ (flip1 * go)
    st[KY_] = ky ^ (flip2 * go)


def plan_round(st, plan, r, gy):
    nz, ny, z, y = st[NZ_], st[NY_], st[Z_], st[Y_]
    kz, ky, loc, ready = st[KZ_], st[KY_], st[LOC_], st[READY_]
    rowid = lax.broadcasted_iota(jnp.int32, (64, 512), 0)
    lane = lax.broadcasted_iota(jnp.int32, (8, 128), 1)
    mine = (rowid[:, :1] & 15) == gy
    usez = jnp.logical_and(nz > 0, jnp.logical_or(st[FIRST_] == 0, ny == 0))
    dist = nz + ny
    active = jnp.logical_and(dist > 0, ready <= r)
    k = jnp.where(usez, kz, ky + 2)
    key = jnp.where(active, k * 16 + y * 4 + z, -1)
    score = dist * 512 + loc + 1
    key = jnp.concatenate([key] * 8, axis=0)
    wide = jnp.concatenate([score] * 8, axis=0)
    bids = jnp.where(rowid == key, wide, 0)
    best = jnp.maximum(jnp.max(bids, axis=1, keepdims=True), 1)
    won = jnp.where(bids == best, 1, 0)
    moved = won[0:8]
    for i in range(1, 8):
        moved = jnp.maximum(moved, won[8 * i : 8 * i + 8])
    moved = jnp.broadcast_to(jnp.max(moved, axis=0, keepdims=True), STATE)
    own = jnp.where(mine, best, 0)
    line = jnp.zeros((8, 128), jnp.int32)
    for i in range(4):
        chosen = jnp.max(own[16 * i : 16 * i + 16], axis=0, keepdims=True)
        line = jnp.where(lane == i, jnp.broadcast_to(chosen, (8, 128)), line)
    plan[r] = jnp.maximum(line - 1, 0) & 511
    wentz = jnp.where(usez, moved, 0)
    wenty = moved - wentz
    st[NZ_] = nz - wentz
    st[NY_] = ny - wenty
    st[Z_] = (z + wentz * (1 - 2 * kz)) & 3
    st[Y_] = (y + wenty * (1 - 2 * ky)) & 3
    st[LOC_] = jnp.where(moved == 1, OWN + 4 * r + k, loc)
    st[READY_] = jnp.where(moved == 1, r + 1 + DELAY, ready)


def close_plan(tiles, st, last, flags, gx, gy):
    _, _, piece = lanes_of()
    live, dest, slot = decode_tiles(tiles)
    row = lax.broadcasted_iota(jnp.int32, STATE, 0)
    wanted = jnp.logical_and(live, jnp.logical_and(dest == gy, slot == row))
    for i in range(PIECES):
        found = jnp.where(jnp.logical_and(wanted, piece == i), st[LOC_], 0)
        last[8 * i : 8 * i + 8, :] = jnp.broadcast_to(jnp.max(found, axis=1, keepdims=True), (8, 128))
    left = jnp.max(st[NZ_] + st[NY_], axis=1, keepdims=True)
    flags[gx] = jnp.broadcast_to(left, (8, 128))


def step_kernel(
    owner, fields, incr, flow, mailed, own_codes, unfinished, F, NZ, FL, CT, xs, ye, ys, yr, pool, landing, leaving,
    shelf, tiles, st, plan, last, flags, plan_s, last_s, flags_s,
    lsem, hs, hr, tsend, trecv, fsend, frecv, msem, psem, ssem, rsem, osem,
):
    gx, gy = lax.axis_index("gx"), lax.axis_index("gy")
    edges, flows, block, noise = start_loads(fields, incr, flow, F, NZ, FL, xs, ye, lsem)
    barrier = pltpu.get_barrier_semaphore()
    row_peers = [lax.rem(gy + i, 16) for i in range(1, 16)]
    col_peers = [lax.rem(gx + i, 8) for i in range(1, 8)]
    for peer in row_peers:
        pl.semaphore_signal(barrier, inc=1, device_id=(gx, peer), device_id_type=MESH)
    for peer in col_peers:
        pl.semaphore_signal(barrier, inc=1, device_id=(peer, gy), device_id_type=MESH)
    tiles[gy] = make_tile(owner, gy)
    pl.semaphore_wait(barrier, 22)
    mail = []
    for i, peer in enumerate(row_peers):
        mail.append(
            pltpu.make_async_remote_copy(
                tiles.at[gy], tiles.at[gy], tsend.at[i], trecv.at[i],
                device_id=(gx, peer), device_id_type=MESH,
            )
        )
    for copy in mail:
        copy.start()
    for copy in edges:
        copy.wait()
    mask_edges(owner, xs, ye, ys)
    halos = halo_copies(F, xs, ys, yr, hs, hr)
    for copy in halos:
        copy.start()
    F2 = F.reshape(2, 68 * PITCH, 128)
    for copy in flows:
        copy.wait()
    make_coefficients(FL, CT)
    for copy in block:
        copy.wait()
    mask_block(owner, F2)
    for copy in noise:
        copy.wait()

    def compute(batch):
        def packet(i, carry):
            b, piece = packet_of(batch, i)
            row, col = b // 4, lax.rem(b, 4)
            for odd in range(2):

                @pl.when(lax.rem(piece, 2) == odd)
                def _():
                    for step in range(8):
                        coded = brick_line(F2, NZ, CT, row, col, piece // 2, 8 * odd + step)
                        for comp in range(2):
                            pool[PIECES * b + piece, pl.ds(32 * step, 32), pl.ds(128 * comp, 128)] = coded[comp]

            return carry

        lax.fori_loop(0, 4, packet, 0)

    y, z = gy // 4, lax.rem(gy, 4)
    targets = [
        4 * y + lax.rem(z + 1, 4),
        4 * y + lax.rem(z + 3, 4),
        4 * lax.rem(y + 1, 4) + z,
        4 * lax.rem(y + 3, 4) + z,
    ]

    def row_copy(r):
        return pltpu.make_async_copy(plan.at[r], plan_s.at[r], psem.at[r])

    def hop(r, k):
        side = lax.rem(r, DELAY + 1)
        return pltpu.make_async_remote_copy(
            leaving.at[side, k], landing.at[r, k], ssem.at[side, k], rsem.at[r, k],
            device_id=(gx, targets[k]), device_id_type=MESH,
        )

    def collect(r):
        for k in range(4):
            copy = hop(r, k)
            copy.wait()
            pool[OWN + 4 * r + k] = landing[r, k]

    def send(r):
        side = lax.rem(r, DELAY + 1)
        row_copy(r).wait()
        for k in range(4):
            leaving[side, k] = pool[slot_in_pool(plan_s[r, 0, k])]
            hop(r, k).start()

    def ahead(r, steps):
        for i in range(steps):
            balance(st, 3 * r + FIRST_SEARCH + i)
        plan_round(st, plan, r + 1, gy)
        row_copy(r + 1).start()

    def search(t, carry):
        balance(st, t)
        return carry

    def opening(j, carry):
        compute(j)

        @pl.when(j == 0)
        def _():
            for copy in mail:
                copy.wait()
            open_plan(tiles, st)
            lax.fori_loop(0, FIRST_SEARCH, search, 0)
            plan_round(st, plan, 0, gy)
            row_copy(0).start()

        return carry

    lax.fori_loop(0, 2, opening, 0)

    def early(r, carry):
        @pl.when(r > DELAY)
        def _():
            collect(r - DELAY - 1)

        send(r)
        ahead(r, SEARCH)
        compute(r + 2)

        @pl.when(r == 0)
        def _():
            for copy in halos:
                copy.wait()
            unpack_halo(F2, yr)

        return carry

    lax.fori_loop(0, 6, early, 0)
    keep = pltpu.make_async_copy(pool.at[pl.ds(0, OWN)], own_codes, msem.at[2])
    keep.start()

    def later(r, carry):
        collect(r - DELAY - 1)
        send(r)
        ahead(r, 3)
        return carry

    lax.fori_loop(6, ROUNDS - 1, later, 0)
    collect(ROUNDS - DELAY - 2)
    send(ROUNDS - 1)
    close_plan(tiles, st, last, flags, gx, gy)
    news = [
        pltpu.make_async_remote_copy(
            flags.at[gx], flags.at[gx], fsend.at[i], frecv.at[i],
            device_id=(peer, gy), device_id_type=MESH,
        )
        for i, peer in enumerate(col_peers)
    ]
    for copy in news:
        copy.start()
    final = pltpu.make_async_copy(last, last_s, msem.at[0])
    final.start()
    for r in range(ROUNDS - DELAY - 1, ROUNDS):
        collect(r)
    final.wait()

    def deliver(s, carry):
        for i in range(PIECES):
            shelf[PIECES * s + i] = pool[slot_in_pool(last_s[8 * i + s, 0])]
        part = pl.ds(PIECES * s, PIECES)
        pltpu.make_async_copy(shelf.at[part], mailed.at[part], osem.at[s]).start()
        return carry

    lax.fori_loop(0, CAPACITY, deliver, 0)
    for copy in news:
        copy.wait()
    tell = pltpu.make_async_copy(flags, flags_s, msem.at[1])
    tell.start()
    for s in range(CAPACITY):
        part = pl.ds(PIECES * s, PIECES)
        pltpu.make_async_copy(shelf.at[part], mailed.at[part], osem.at[s]).wait()
    keep.wait()
    tell.wait()
    left = flags_s[0, 0, 0]
    for g in range(1, 8):
        left = jnp.maximum(left, flags_s[g, 0, 0])
    unfinished[0] = left


def advance(fields, increments, flow_field, brick_owner):
    any_ = pl.BlockSpec(memory_space=pl.ANY)
    packet = (EDGE * EDGE // PIECES, 256)
    dma = pltpu.SemaphoreType.DMA
    return pl.pallas_call(
        step_kernel,
        out_shape=(
            jax.ShapeDtypeStruct((CAPACITY * PIECES, *packet), jnp.int16),
            jax.ShapeDtypeStruct((OWN, *packet), jnp.int16),
            jax.ShapeDtypeStruct((1,), jnp.int32),
        ),
        in_specs=[pl.BlockSpec(memory_space=pltpu.SMEM), any_, any_, any_],
        out_specs=(any_, any_, pl.BlockSpec(memory_space=pltpu.SMEM)),
        scratch_shapes=[
            pltpu.VMEM((2, 68, PITCH, 128), jnp.float32),
            pltpu.VMEM((NX, NY, 256), jnp.bfloat16),
            pltpu.VMEM((6, NX, NY), jnp.float32),
            pltpu.VMEM((4, 128, 128), jnp.float32),
            pltpu.VMEM((2, 2, 2, NY, 128), jnp.float32),
            pltpu.VMEM((2, 2, NX, 8, 128), jnp.float32),
            pltpu.VMEM((2, 2, 2, NX, 128), jnp.float32),
            pltpu.VMEM((2, 2, 2, NX, 128), jnp.float32),
            pltpu.VMEM((OWN + 4 * ROUNDS, *packet), jnp.int16),
            pltpu.VMEM((ROUNDS, 4, *packet), jnp.int16),
            pltpu.VMEM((DELAY + 1, 4, *packet), jnp.int16),
            pltpu.VMEM((CAPACITY * PIECES, *packet), jnp.int16),
            pltpu.VMEM((16, 8, 128), jnp.int32),
            pltpu.VMEM((9, *STATE), jnp.int32),
            pltpu.VMEM((ROUNDS, 8, 128), jnp.int32),
            pltpu.VMEM((8 * PIECES, 128), jnp.int32),
            pltpu.VMEM((8, 8, 128), jnp.int32),
            pltpu.SMEM((ROUNDS, 8, 128), jnp.int32),
            pltpu.SMEM((8 * PIECES, 128), jnp.int32),
            pltpu.SMEM((8, 8, 128), jnp.int32),
            dma((12,)),
            dma((4,)),
            dma((4,)),
            dma((15,)),
            dma((15,)),
            dma((7,)),
            dma((7,)),
            dma((3,)),
            dma((ROUNDS,)),
            dma((DELAY + 1, 4)),
            dma((ROUNDS, 4)),
            dma((CAPACITY,)),
        ],
        compiler_params=pltpu.CompilerParams(
            collective_id=0, has_side_effects=True, vmem_limit_bytes=58 * 2**20
        ),
    )(brick_owner, fields, increments, flow_field)


def finish_kernel(source, codes, out):
    out[0] = decode(codes[0]).reshape(out.shape[1:])


def finish(source, arrived, slots):
    return pl.pallas_call(
        finish_kernel,
        out_shape=jax.ShapeDtypeStruct((slots, EDGE, EDGE, 256), jnp.float32),
        grid_spec=pltpu.PrefetchScalarGridSpec(
            num_scalar_prefetch=1,
            grid=(slots, 2),
            in_specs=[pl.BlockSpec((1, 512, 256), lambda s, h, source: (source[s], h, 0))],
            out_specs=pl.BlockSpec((1, 16, EDGE, 256), lambda s, h, source: (s, h, 0, 0)),
        ),
        compiler_params=pltpu.CompilerParams(vmem_limit_bytes=32 * 2**20),
    )(source, arrived)


def pick_kernel(chosen, codes, out):
    out[...] = codes[...]


def pick(chosen, codes, peers):
    block = (1, EDGE * EDGE, 256)
    return pl.pallas_call(
        pick_kernel,
        out_shape=jax.ShapeDtypeStruct((peers, EDGE * EDGE, 256), jnp.int16),
        grid_spec=pltpu.PrefetchScalarGridSpec(
            num_scalar_prefetch=1,
            grid=(peers,),
            in_specs=[pl.BlockSpec(block, lambda s, chosen: (chosen[s], 0, 0))],
            out_specs=pl.BlockSpec(block, lambda s, chosen: (s, 0, 0)),
        ),
        compiler_params=pltpu.CompilerParams(vmem_limit_bytes=32 * 2**20),
    )(chosen, codes)


def dense(codes, owner_table, brick_owner):
    peer_count = lax.axis_size("gy")
    device = lax.axis_index("gx") * peer_count + lax.axis_index("gy")
    owner_flat = brick_owner.reshape(8)
    target = jnp.where(owner_flat >= 0, owner_flat // CAPACITY % peer_count, -1)
    match_grid = target[None, :] == jnp.arange(peer_count, dtype=jnp.int32)[:, None]
    chosen = jnp.sum(jnp.where(match_grid, jnp.arange(8, dtype=jnp.int32)[None, :], 0), axis=1)
    wanted = device * CAPACITY + jnp.arange(CAPACITY, dtype=jnp.int32)
    column = jnp.arange(owner_table.shape[1], dtype=jnp.int32)
    found = owner_table[None, :, :] == wanted[:, None, None]
    source = jnp.sum(jnp.where(found, (column // 4)[None, None, :], 0), axis=(1, 2))
    picked = pick(chosen, codes.reshape(8, EDGE * EDGE, 256), peer_count)
    arrived = lax.all_to_all(picked, "gy", split_axis=0, concat_axis=0, tiled=True)
    return finish(source, arrived, CAPACITY)


def spread_kernel(codes, out, taken, made, isem, osem):
    packets = CAPACITY * PIECES

    def arrive(i):
        return pltpu.make_async_copy(codes.at[pl.ds(2 * i, 2)], taken.at[pl.ds(2 * i, 2)], isem.at[i])

    def leave(i):
        return pltpu.make_async_copy(made.at[i], out.at[i // 2, pl.ds(16 * lax.rem(i, 2), 16)], osem.at[i])

    for i in range(packets // 2):
        arrive(i).start()

    def half(i, carry):
        arrive(i).wait()
        for j in range(2):
            made[i, pl.ds(8 * j, 8)] = decode(taken[2 * i + j]).reshape(8, EDGE, 256)
        leave(i).start()
        return carry

    lax.fori_loop(0, packets // 2, half, 0)
    for i in range(packets // 2):
        leave(i).wait()


def spread(mailed):
    packets = CAPACITY * PIECES
    return pl.pallas_call(
        spread_kernel,
        out_shape=jax.ShapeDtypeStruct((CAPACITY, EDGE, EDGE, 256), jnp.float32),
        in_specs=[pl.BlockSpec(memory_space=pl.ANY)],
        out_specs=pl.BlockSpec(memory_space=pl.ANY),
        scratch_shapes=[
            pltpu.VMEM((packets, EDGE * EDGE // PIECES, 256), jnp.int16),
            pltpu.VMEM((packets // 2, 16, EDGE, 256), jnp.float32),
            pltpu.SemaphoreType.DMA((packets // 2,)),
            pltpu.SemaphoreType.DMA((packets // 2,)),
        ],
        compiler_params=pltpu.CompilerParams(vmem_limit_bytes=60 * 2**20),
    )(mailed)


def on_device(fields, increments, flow_field, brick_owner):
    mailed, codes, unfinished = advance(fields, increments, flow_field, brick_owner)

    def routed():
        return spread(mailed)

    def fallback():
        owner_table = lax.all_gather(brick_owner, "gy", axis=1, tiled=True)
        return dense(codes, owner_table, brick_owner)

    return lax.cond(unfinished[0] == 0, routed, fallback)


def solution(mesh):
    in_specs = (P("gx", "gy", None), P("gx", "gy", None), P(None, "gx", "gy"), P("gx", "gy"))
    out_specs = P(("gx", "gy"), None, None, None)
    return jax.shard_map(
        on_device, mesh=mesh, in_specs=in_specs, out_specs=out_specs, check_vma=False
    )
```
